128 devices in a mesh: seq: 8 (over z, core), ctx: 8 (over x, y_hi), tp: 2 (over y_lo).
Axes of the slice: x: 4, y: 4 (y_hi: 2, y_lo: 2; y = y_hi * 2 + y_lo), z: 4, core: 2. Of those that a mesh axis runs over, the one named last changes fastest.
Arguments:
- tokens: bfloat16 [8, 2048, 1024], P('seq', 'ctx'), may hold values from -6 to 6
- positions: int32 [8, 2048], P('seq', 'ctx'), may hold values from 0 to 2047, as said below
- cotangent: bfloat16 [8, 2048, 1024], P('seq', 'ctx'), may hold values from -6 to 6
- ln_gain: float32 [1024], replicated, may hold values from 0.5 to 1.5
- ln_bias: float32 [1024], replicated, may hold values from -3 to 3
- qkv_weight: bfloat16 [1024, 3, 1024], P(None, None, 'tp'), may hold values from -0.1875 to 0.1875
- out_weight: bfloat16 [1024, 1024], P('tp'), may hold values from -2 to 2
- fc_in_weight: bfloat16 [1024, 4096], P(None, 'tp'), may hold values from -0.1875 to 0.1875
- fc_in_bias: float32 [4096], P('tp'), may hold values from -3 to 3
- fc_out_weight: bfloat16 [4096, 1024], P('tp'), may hold values from -0.09375 to 0.09375
- fc_out_bias: float32 [1024], replicated, may hold values from -3 to 3
Outputs:
- block_out: bfloat16 [8, 2048, 1024], P('seq', 'ctx')
- tokens_grad: float32 [8, 2048, 1024], P('seq', 'ctx')
- ln_gain_grad: float32 [1024], replicated
- ln_bias_grad: float32 [1024], replicated
- qkv_grad: float32 [1024, 3, 1024], P(None, None, 'tp')
- out_grad: float32 [1024, 1024], P('tp')
- fc_in_grad: float32 [1024, 4096], P(None, 'tp')
- fc_in_bias_grad: float32 [4096], P('tp')
- fc_out_grad: float32 [4096, 1024], P('tp')
- fc_out_bias_grad: float32 [1024], replicated
The draws below stay inside these ranges and needn't reach their ends.
Inputs may be any that keep to these rules, and one draw needn't show every extreme that they name: Each sequence's positions take every value of 0 to 2047 once; the 256 positions on one device are consecutive and rising, starting at a multiple of 256.
All inputs are finite; a program needn't handle non-finite values.
Results may differ from the reference program's by a relative error of at most 0.023.
Values may be sent and summed in bfloat16 or wider, within the bound.
A program may use at most 256 MiB of HBM per device.

```python
import math
import jax
import jax.numpy as jnp
from jax import lax

D = 1024
H = 16
HD = 64
ROT = 32
FF = 4096
BLK = 256
NSEQ = 8
LEN = 2048


def block_order(one_key):
    return jax.random.permutation(one_key, LEN // BLK)


def draw_positions(key, part):
    key = jax.random.fold_in(key, 7)
    seq_keys = jax.random.split(key, NSEQ)
    orders = jax.vmap(block_order)(seq_keys).astype(jnp.int32)
    offsets = jnp.arange(BLK, dtype=jnp.int32)
    places = orders[:, :, None] * BLK + offsets[None, None, :]
    return places.reshape(NSEQ, LEN).astype(jnp.int32)


def block_levels(stream_key, extent, cuts, low, largest):
    loudness = 1.0
    for position, parts in cuts:
        draws = jax.random.uniform(jax.random.fold_in(jax.random.fold_in(stream_key, 6), position), (parts,), jnp.float32, low / len(cuts), largest / len(cuts))
        loudness = loudness * jnp.repeat(jnp.exp(draws), extent[position] // parts).reshape((-1,) + (1,) * (len(extent) - 1 - position))
    return loudness


def scatter_about(rng, extent, scale, limit, cuts=(), kind=jnp.bfloat16):
    level = block_levels(rng, extent, cuts, -0.22, 0.18) if cuts else 1.0
    values = jax.random.normal(rng, extent, jnp.float32) * scale * level
    return jnp.minimum(jnp.maximum(values, -limit), limit).astype(kind)


def setup_inputs(seed: int = 0) -> dict:
    splits = jax.random.split(jax.random.key(seed), 12)
    tokens = scatter_about(splits[0], (NSEQ, LEN, D), 1.0, 6.0, ((0, 8), (1, 8)))
    positions = draw_positions(jax.random.fold_in(splits[11], 71), 0)
    cotangent = scatter_about(splits[2], (NSEQ, LEN, D), 1.0, 6.0, ((0, 8), (1, 8)))
    ln_gain = jnp.clip(jax.random.uniform(splits[3], (D,), jnp.float32, 0.5, 1.5), 0.5, 1.5)
    ln_bias = scatter_about(splits[4], (D,), 0.5, 3.0, (), jnp.float32)
    qkv_weight = scatter_about(splits[5], (D, 3, D), D ** -0.5, 0.1875, ((2, 2),))
    out_weight = scatter_about(splits[6], (D, D), (max(1, 16 * D // LEN)) ** -0.5, 2.0, ((0, 2),))
    fc_in_weight = scatter_about(splits[7], (D, FF), D ** -0.5, 0.1875, ((1, 2),))
    fc_in_bias = scatter_about(splits[8], (FF,), 0.5, 3.0, ((0, 2),), jnp.float32)
    fc_out_weight = scatter_about(splits[9], (FF, D), FF ** -0.5, 0.09375, ((0, 2),))
    fc_out_bias = scatter_about(splits[10], (D,), 0.5, 3.0, (), jnp.float32)
    return {"tokens": tokens, "positions": positions, "cotangent": cotangent, "ln_gain": ln_gain, "ln_bias": ln_bias, "qkv_weight": qkv_weight, "out_weight": out_weight, "fc_in_weight": fc_in_weight, "fc_in_bias": fc_in_bias, "fc_out_weight": fc_out_weight, "fc_out_bias": fc_out_bias}


@jax.custom_vjp
def low(v):
    return lax.optimization_barrier(v.astype(jnp.bfloat16)).astype(jnp.float32)

@jax.custom_vjp
def low_back(v):
    return v

def low_keep(v):
    return (low(v), None)

def low_pass(kept, grad):
    return (grad,)

def back_keep(v):
    return (v, None)

def back_low(kept, grad):
    return (low(grad),)
low.defvjp(low_keep, low_pass)
low_back.defvjp(back_keep, back_low)
highest = lax.Precision.HIGHEST
eps_norm = 1e-05

def angle_tables(places):
    frequency = jnp.exp(jnp.arange(ROT // 2, dtype=jnp.float32) * (-2.0 * math.log(10000.0) / ROT))
    turned = places.astype(jnp.float32)[:, None] * frequency[None, :]
    return (jnp.cos(turned)[:, None, :], jnp.sin(turned)[:, None, :])

def rotate(vectors, cosine, sine_table):
    lead_shape = vectors.shape[:-1]
    paired = vectors[..., :ROT].reshape(lead_shape + (ROT // 2, 2))
    first_part = paired[..., 0]
    second_part = paired[..., 1]
    turned = jnp.stack([first_part * cosine - second_part * sine_table, second_part * cosine + first_part * sine_table], axis=-1)
    return jnp.concatenate([turned.reshape(lead_shape + (ROT,)), vectors[..., ROT:]], axis=-1)

def attend_block(query_block, place_block, key_rot, value_rot, key_places):
    scores = jnp.einsum('qhd,khd->hqk', query_block, key_rot, precision=highest) * HD ** (-0.5)
    scores = low_back(scores)
    allowed = key_places[None, :] <= place_block[:, None]
    scores = jnp.where(allowed[None], scores, -1e+30)
    row_max = lax.optimization_barrier(jnp.max(scores, axis=-1, keepdims=True))
    expo_terms = jnp.exp(scores - row_max)
    prob_low = low(expo_terms / lax.optimization_barrier(jnp.sum(expo_terms, axis=-1, keepdims=True)))
    return jnp.einsum('hqk,khd->qhd', prob_low, value_rot, precision=highest)

def layer(inputs, places, weights):
    ln_gain, ln_bias, qkv_weight, out_weight, fc_in_weight, fc_in_bias, fc_out_weight, fc_out_bias = weights
    length = inputs.shape[0]
    mean_value = lax.optimization_barrier(jnp.mean(inputs, axis=-1, keepdims=True))
    centered = inputs - mean_value
    variance = lax.optimization_barrier(jnp.mean(centered * centered, axis=-1, keepdims=True))
    normed = low(centered * lax.rsqrt(variance + eps_norm) * ln_gain + ln_bias)
    projected = jnp.dot(normed, qkv_weight.reshape(D, 3 * D), precision=highest).reshape(length, 3, H, HD)
    cosine, sine_table = angle_tables(places)
    queries = low(rotate(low_back(projected[:, 0]), cosine, sine_table))
    key_rot = low(rotate(low_back(projected[:, 1]), cosine, sine_table))
    value_rot = low(low_back(projected[:, 2]))
    block_rows = math.gcd(length, 512)
    block_count = length // block_rows

    def one_block(block_index):
        row_start = block_index * block_rows
        query_block = lax.dynamic_slice_in_dim(queries, row_start, block_rows, 0)
        place_block = lax.dynamic_slice_in_dim(places, row_start, block_rows, 0)
        return jax.checkpoint(attend_block)(query_block, place_block, key_rot, value_rot, places)
    attended = lax.map(one_block, jnp.arange(block_count, dtype=jnp.int32)).reshape(length, D)
    attended = low(low_back(attended))
    hidden_pre = low_back(jnp.dot(normed, fc_in_weight, precision=highest) + fc_in_bias)
    activated = low(jax.nn.gelu(hidden_pre, approximate=True))
    attn_branch = jnp.dot(attended, out_weight, precision=highest)
    mlp_branch = jnp.dot(activated, fc_out_weight, precision=highest)
    return inputs + attn_branch + mlp_branch + fc_out_bias

def reference(tokens, positions, cotangent, ln_gain, ln_bias, qkv_weight, out_weight, fc_in_weight, fc_in_bias, fc_out_weight, fc_out_bias):
    params = tuple((weight.astype(jnp.float32) for weight in (ln_gain, ln_bias, qkv_weight, out_weight, fc_in_weight, fc_in_bias, fc_out_weight, fc_out_bias)))

    def one_sequence(totals, sequence):
        seq_tokens, seq_places, seq_grad = sequence

        def forward(inputs, weights):
            return layer(inputs, seq_places, weights)
        outputs, pullback = jax.vjp(forward, seq_tokens.astype(jnp.float32), params)
        input_grad, weight_grads = pullback(seq_grad.astype(jnp.float32))
        totals = tuple((total + grad_term for total, grad_term in zip(totals, weight_grads)))
        return (totals, (outputs.astype(jnp.bfloat16), input_grad))
    initial = tuple((jnp.zeros(weight.shape, jnp.float32) for weight in params))
    totals, stacked = lax.scan(one_sequence, initial, (tokens, positions, cotangent))
    block_out, tokens_grad = stacked
    return (block_out, tokens_grad, totals[0], totals[1], totals[2], totals[3], totals[4], totals[5], totals[6], totals[7])
```

```python
import math
from types import SimpleNamespace

import jax
import jax.numpy as jnp
from jax import lax
from jax.experimental import pallas as pl
from jax.experimental.pallas import tpu as pltpu
from jax.sharding import PartitionSpec as P

HD = 64
ROT = 32
T = 256
D = 1024
L = 512
F = 2048
MESH = pl.DeviceIdType.MESH
BF = jnp.bfloat16
F32 = jnp.float32
EPS = 1e-05
SIZES = (512, 256, 128, 64, 32)
OFFS = (0, 512, 768, 896, 960)


def dot(a, b):
    return lax.dot_general(a, b, (((1,), (0,)), ((), ())), preferred_element_type=F32)


def dot_nt(a, b):
    return lax.dot_general(a, b, (((1,), (1,)), ((), ())), preferred_element_type=F32)


def xor(a, b):
    return a + b - 2 * a * b


class Place:
    def __init__(self):
        seq, ctx, tp = lax.axis_index("seq"), lax.axis_index("ctx"), lax.axis_index("tp")
        self.seq, self.ctx, self.tp = seq, ctx, tp
        self.z, self.core, self.x, self.yh = seq // 2, seq % 2, ctx // 2, ctx % 2
        c, x, z = self.core, self.x, self.z
        flip = lambda i: i + 1 - 2 * (i % 2)
        self.sib = (z * 2 + 1 - c, ctx, tp)
        self.other_tp = (seq, ctx, 1 - tp)
        self.y = (seq, x * 2 + 1 - self.yh, tp)
        self.x_one = (seq, flip(x) * 2 + self.yh, tp)
        self.x_three = (seq, (3 - x) * 2 + self.yh, tp)
        self.z_one = (flip(z) * 2 + c, ctx, tp)
        self.z_three = ((3 - z) * 2 + c, ctx, tp)
        pick = lambda a, b: tuple((1 - c) * p + c * q for p, q in zip(a, b))
        u, v = (1 - c) * x + c * z, (1 - c) * z + c * x
        u_one, u_three = pick(self.x_one, self.z_one), pick(self.x_three, self.z_three)
        v_one, v_three = pick(self.z_one, self.x_one), pick(self.z_three, self.x_three)
        u0, u1, v0, v1 = u % 2, u // 2, v % 2, v // 2
        partner = (
            (u_one, u_three, v_one, v_three, self.y),
            (u_three, u_one, v_three, v_one, self.y),
        )
        bits = (
            (xor(u0, u1), u1, xor(v0, v1), v1, self.yh),
            (u1, u0, v1, v0, self.yh),
        )
        self.partner = partner
        self.keep, self.give = [], []
        for half in range(2):
            base, keep, give = 0, [], []
            for step in range(5):
                size, bit = SIZES[step], bits[half][step]
                keep.append(pl.multiple_of(base + bit * size, 32))
                give.append(pl.multiple_of(base + (1 - bit) * size, 32))
                base = base + bit * size
            self.keep.append(keep)
            self.give.append(give)


def remote(src, dst, send, recv, device):
    return pltpu.make_async_remote_copy(
        src_ref=src, dst_ref=dst, send_sem=send, recv_sem=recv, device_id=device, device_id_type=MESH
    )


def rotate(u, cosine, even, odd):
    return u * cosine + pltpu.roll(u, 127, 1) * even + pltpu.roll(u, 1, 1) * odd


def layer_kernel(
    pos, tok_h, cot_h, gain, lnb, wqkv_h, wout_h, fin_h, finb, fout_h, foutb,
    out_b, out_t, out_s, out_r,
    tok, cot, nrm, xhat, inv, wqkv, wout, fin, fout, tabs,
    send1, land1, ptile, pland, psm, qg, kv, kvt, sbuf, pbuf, dkv, aq,
    send2, land2, act_o, act_b, gh_o, gh_b, lf_o, lf_b, nrm_t, cot_t, act_t,
    branch, gnp, tps, tpl, g0, g1, g2, l0, l1, l2, r0, r1, r2, vs, vw,
    in_sem, sib_s, sib_r, a_s, a_r, p_s, p_r, b_s, b_r, tp_s, tp_r,
    rs_s, rs_r, ag_s, ag_r, fw_s, fw_r, st_s, v_s, v_r, ps_sem,
):
    me = Place()
    core, ctx = me.core, me.ctx
    g, lands, res = (g0, g1, g2), (l0, l1, l2), (r0, r1, r2)

    loads = [
        pltpu.make_async_copy(a, b, in_sem.at[i])
        for i, (a, b) in enumerate(
            ((tok_h, tok), (cot_h, cot.at[0]), (wqkv_h, wqkv), (wout_h, wout), (fin_h, fin), (fout_h, fout))
        )
    ]
    for copy in loads:
        copy.start()

    barrier = pltpu.get_barrier_semaphore()
    peers = [(me.seq, lax.rem(ctx + k, 8), me.tp) for k in range(1, 8)]
    for device in peers + [me.sib, me.other_tp, me.z_one, me.z_three]:
        pl.semaphore_signal(barrier, inc=1, device_id=device, device_id_type=MESH)

    first = pos[0, 0]
    lane = lax.broadcasted_iota(jnp.int32, (T, 128), 1)
    row = lax.broadcasted_iota(jnp.int32, (T, 128), 0)
    in_head = lane % HD
    freq = jnp.exp((in_head // 2).astype(F32) * (-2.0 * math.log(10000.0) / ROT))
    theta = (row + first).astype(F32) * freq
    turning = in_head < ROT
    sine = jnp.where(turning, jnp.sin(theta), 0.0)
    tabs[0] = jnp.where(turning, jnp.cos(theta), 1.0)
    tabs[1] = jnp.where(lane % 2 == 0, -sine, 0.0)
    tabs[2] = jnp.where(lane % 2 == 0, 0.0, sine)
    ptile[...] = jnp.full((8, 128), first, jnp.int32)

    loads[0].wait()

    def norm_rows(i, _):
        rows = pl.ds(pl.multiple_of(i * 64, 64), 64)
        x = tok[rows, :].astype(F32)
        x = x - jnp.mean(x, axis=-1, keepdims=True)
        inv_std = lax.rsqrt(jnp.mean(x * x, axis=-1, keepdims=True) + EPS)
        x = x * inv_std
        xhat[rows, :] = x
        inv[rows, :] = jnp.broadcast_to(inv_std, (64, 128))
        nrm[0, rows, :] = (x * gain[...] + lnb[...]).astype(BF)
        return 0

    lax.fori_loop(0, T // 64, norm_rows, 0)

    loads[1].wait()
    pl.semaphore_wait(barrier, 11)
    sib = [None] * 5
    sib[0] = remote(cot.at[0], cot.at[1], sib_s.at[0], sib_r.at[0], me.sib)
    sib[1] = remote(nrm.at[0], nrm.at[1], sib_s.at[1], sib_r.at[1], me.sib)
    sib[0].start()
    sib[1].start()

    loads[2].wait()
    loads[3].wait()
    normed = nrm[0]
    low_lane = lane < HD

    def lanes(e):
        return slice(128 * e, 128 * e + 128)

    for e in range(4):
        cols = slice(128 * e, 128 * e + 128)
        turn = (tabs[0], tabs[1], tabs[2])
        q = rotate(dot(normed, wqkv[0, :, cols]), *turn) * HD ** (-0.5)
        k = rotate(dot(normed, wqkv[1, :, cols]), *turn)
        v = dot(normed, wqkv[2, :, cols])
        ga = dot_nt(cot[0], wout[128 * e : 128 * e + 128, :])
        swap = lambda a: pltpu.roll(a, HD, 1)
        send1[2 * e, :, 0:128] = jnp.where(low_lane, q, swap(ga)).astype(BF)
        send1[2 * e, :, 128:256] = jnp.where(low_lane, k, swap(v)).astype(BF)
        send1[2 * e + 1, :, 0:128] = jnp.where(low_lane, swap(q), ga).astype(BF)
        send1[2 * e + 1, :, 128:256] = jnp.where(low_lane, swap(k), v).astype(BF)
    first_out, place_out = [], []
    for k in range(1, 8):
        to = lax.rem(ctx + k, 8)
        place_out.append(remote(ptile, pland.at[ctx], p_s.at[k - 1], p_r.at[k - 1], peers[k - 1]))
        first_out.append(remote(send1.at[to], land1.at[ctx], a_s.at[k - 1], a_r.at[k - 1], peers[k - 1]))
    for copy in place_out + first_out:
        copy.start()
    land1[ctx] = send1[ctx]
    pland[ctx] = ptile[...]

    loads[4].wait()
    loads[5].wait()
    vs[0] = jnp.zeros((8, D), F32)

    def hidden(half, act_ref, gh_ref, i):
        start = pl.multiple_of(half * 1024 + i * 256, 256)
        here = pl.ds(pl.multiple_of(i * 256, 256), 256)
        u = dot(nrm[0], fin[:, pl.ds(start, 256)]) + finb[:, pl.ds(start, 256)]
        z = math.sqrt(2.0 / math.pi) * (u + 0.044715 * u * u * u)
        t = jnp.tanh(z)
        act_ref[:, here] = (0.5 * u * (1.0 + t)).astype(BF)
        slope = 0.5 * (1.0 + t) + (0.5 * math.sqrt(2.0 / math.pi)) * u * (1.0 - t * t) * (
            1.0 + 3 * 0.044715 * u * u
        )
        grad = dot_nt(cot[0], fout[pl.ds(start, 256), :]) * slope
        low = grad.astype(BF)
        gh_ref[:, here] = low
        vs[0, pl.ds(2 + half, 1), here] = jnp.sum(low.astype(F32), axis=0, keepdims=True)

    def other_half(i, _):
        hidden(1 - core, act_o, gh_o, i)
        return 0

    def own_half(i, _):
        hidden(core, act_b.at[0], gh_b.at[0], i)
        return 0

    lax.fori_loop(0, 4, other_half, 0)
    sib[2] = remote(act_o, act_b.at[1], sib_s.at[2], sib_r.at[2], me.sib)
    sib[3] = remote(gh_o, gh_b.at[1], sib_s.at[3], sib_r.at[3], me.sib)
    sib[2].start()
    sib[3].start()
    lax.fori_loop(0, 4, own_half, 0)
    vs[0, 4:5, :] = jnp.sum(cot[0].astype(F32), axis=0, keepdims=True)

    sib[0].wait_recv()
    sib[1].wait_recv()

    def turn_over(src, dst):
        def body(i, _):
            here = pl.ds(pl.multiple_of(i * 128, 128), 128)
            for token in range(2):
                dst[here, token * T : token * T + T] = src[token, :, here].T
            return 0

        lax.fori_loop(0, D // 128, body, 0)

    turn_over(nrm, nrm_t)
    turn_over(cot, cot_t)
    sib[2].wait_recv()
    turn_over(act_b, act_t)

    def outer(left_t, right, dest):
        def body(i, _):
            rows = pl.ds(pl.multiple_of(i * 128, 128), 128)
            a0, a1 = left_t[rows, 0:T], left_t[rows, T : 2 * T]
            for half in range(2):
                b = slice(512 * half, 512 * half + 512)
                dest[half, rows, :] = (dot(a0, right[0, :, b]) + dot(a1, right[1, :, b])).astype(BF)
            return 0

        lax.fori_loop(0, D // 128, body, 0)

    def rs_copy(m, h, s):
        return remote(
            g[m].at[h, pl.ds(me.give[h][s], SIZES[s])],
            lands[m].at[h, pl.ds(OFFS[s], SIZES[s])],
            rs_s.at[m, h, s],
            rs_r.at[m, h, s],
            me.partner[h][s],
        )

    def ag_copy(m, h, s):
        rows = pl.ds(me.keep[h][s], SIZES[s])
        return remote(
            res[m].at[h, rows], res[m].at[h, rows], ag_s.at[m, h, s], ag_r.at[m, h, s], me.partner[h][s]
        )

    def fw_copy(m, h, s):
        rows = pl.ds((me.keep if s == 0 else me.give)[h][0], SIZES[0])
        return remote(
            res[m].at[h, rows], out_r.at[m, core, h, rows], fw_s.at[m, h, s], fw_r.at[m, h, s], me.sib
        )

    def st_copy(m, h, s):
        rows = pl.ds((me.keep if s == 0 else me.give)[h][0], SIZES[0])
        return pltpu.make_async_copy(res[m].at[h, rows], out_r.at[m, core, h, rows], st_s.at[m, h, s])

    def rs_start(m):
        for h in range(2):
            rs_copy(m, h, 0).start()

    def rs_step(m, s):
        size = SIZES[s]
        block = min(size, 64)
        for h in range(2):
            rs_copy(m, h, s).wait_recv()

            def body(i, _):
                here = pl.ds(pl.multiple_of(me.keep[h][s] + i * block, 32), block)
                there = pl.ds(pl.multiple_of(OFFS[s] + i * block, 32), block)
                total = g[m][h, here, :].astype(F32) + lands[m][h, there, :].astype(F32)
                (g if s < 4 else res)[m][h, here, :] = total.astype(BF)
                return 0

            lax.fori_loop(0, size // block, body, 0)
            if s < 4:
                rs_copy(m, h, s + 1).start()
            else:
                ag_copy(m, h, 4).start()

    def ag_step(m, s):
        for h in range(2):
            ag_copy(m, h, s).wait_recv()
            if s > 0:
                ag_copy(m, h, s - 1).start()
            if s == 1:
                fw_copy(m, h, 0).start()
                st_copy(m, h, 0).start()
            if s == 0:
                fw_copy(m, h, 1).start()
                st_copy(m, h, 1).start()

    outer(act_t, cot, g0)
    rs_start(0)
    sib[3].wait_recv()
    outer(nrm_t, gh_b, g1)
    rs_start(1)

    for copy in place_out:
        copy.wait_recv()
    to_scalar = pltpu.make_async_copy(pland, psm, ps_sem)
    to_scalar.start()
    for copy in first_out:
        copy.wait_recv()
    to_scalar.wait()
    rank = [psm[c, 0, 0] // T for c in range(8)]
    for r in range(8):
        at = 0
        for c in range(8):
            at = jnp.where(rank[c] == r, c, at)
        block = land1[at]
        rows = slice(r * T, r * T + T)
        qg[rows, :] = block[:, 0:128]
        kv[rows, :] = block[:, 128:256]
        kvt[:, rows] = block[:, 128:256].T

    dkv[...] = jnp.zeros_like(dkv)

    def attend(r):
        qgr = qg[r * T : r * T + T, :]
        zero = jnp.zeros_like(qgr)
        lower = lax.broadcasted_iota(jnp.int32, (T, 128), 1) < HD
        q = jnp.where(lower, qgr, zero)
        ga = jnp.where(lower, zero, qgr)
        ga_t = qgr.T[HD:, :].astype(F32)

        def key(j):
            return pl.ds(pl.multiple_of(j * T, T), T)

        def scores(j, top):
            s = dot_nt(kv[key(j), :], q)
            sbuf[key(j), :] = s
            return jnp.maximum(top, jnp.max(s.reshape(T // 8, 8, T), axis=0))

        top = lax.fori_loop(0, r, scores, jnp.full((8, T), -1e30, F32))
        s = dot_nt(kv[key(r), :], q)
        below = lax.broadcasted_iota(jnp.int32, (T, T), 0) <= lax.broadcasted_iota(jnp.int32, (T, T), 1)
        s = jnp.where(below, s, -1e30)
        sbuf[key(r), :] = s
        top = jnp.maximum(top, jnp.max(s.reshape(T // 8, 8, T), axis=0))
        top = jnp.max(top, axis=0, keepdims=True)

        def expo(j, total):
            e = jnp.exp(sbuf[key(j), :] - top)
            sbuf[key(j), :] = e
            return total + jnp.sum(e.reshape(T // 8, 8, T), axis=0)

        total = lax.fori_loop(0, r + 1, expo, jnp.zeros((8, T), F32))
        scale = 1.0 / jnp.sum(total, axis=0, keepdims=True)

        def weigh(j, att):
            prob = (sbuf[key(j), :] * scale).astype(BF)
            pbuf[key(j), :] = prob
            return att + dot(kvt[HD:, key(j)], prob)

        att = lax.fori_loop(0, r + 1, weigh, jnp.zeros((HD, T), F32))
        delta = jnp.sum(ga_t * att, axis=0, keepdims=True)

        def back(j, dq):
            dp = dot_nt(kv[key(j), :], ga)
            ds = (sbuf[key(j), :] * scale * (dp - delta)).astype(BF)
            dkv[key(j), :] += dot(ds, q) + dot(pbuf[key(j), :], ga)
            return dq + dot(kvt[:HD, key(j)], ds)

        dq = lax.fori_loop(0, r + 1, back, jnp.zeros((HD, T), F32))
        both = jnp.concatenate([att, dq * HD ** (-0.5)], axis=0)
        aq[r, :, 0:128] = both.T.astype(BF)
        aq[r, :, 128:256] = dkv[r * T : r * T + T, :].astype(BF)

    attend(7)
    attend(6)
    rs_step(0, 0)
    attend(5)
    rs_step(1, 0)
    attend(4)
    rs_step(0, 1)
    attend(3)
    rs_step(1, 1)
    rs_step(0, 2)
    attend(2)
    rs_step(1, 2)
    rs_step(0, 3)
    attend(1)
    attend(0)

    for c in range(8):
        send2[c] = aq[rank[c]]
    second_out = []
    for k in range(1, 8):
        to = lax.rem(ctx + k, 8)
        second_out.append(remote(send2.at[to], land2.at[ctx], b_s.at[k - 1], b_r.at[k - 1], peers[k - 1]))
    for copy in second_out:
        copy.start()
    land2[ctx] = send2[ctx]
    rs_step(1, 3)
    rs_step(0, 4)
    rs_step(1, 4)

    own, oth = pl.multiple_of(core * 1024, 1024), pl.multiple_of((1 - core) * 1024, 1024)

    def mixed(i, _):
        cols = pl.ds(pl.multiple_of(i * 256, 256), 256)
        branch[:, cols] = dot(act_b[0], fout[pl.ds(own, 1024), cols]) + dot(act_o[...], fout[pl.ds(oth, 1024), cols])
        gnp[:, cols] = dot_nt(gh_b[0], fin[cols, pl.ds(own, 1024)]) + dot_nt(gh_o[...], fin[cols, pl.ds(oth, 1024)])
        return 0

    lax.fori_loop(0, 4, mixed, 0)
    ag_step(0, 4)
    ag_step(1, 4)
    ag_step(0, 3)
    ag_step(1, 3)

    for copy in second_out:
        copy.wait_recv()

    def gather_heads(half, ref):
        for e in range(2):
            here = slice(128 * e, 128 * e + 128)
            low, high = 4 * half + 2 * e, 4 * half + 2 * e + 1
            t0, t1 = land2[low, :, 0:128].astype(F32), land2[high, :, 0:128].astype(F32)
            t2, t3 = land2[low, :, 128:256].astype(F32), land2[high, :, 128:256].astype(F32)
            swap = lambda a: pltpu.roll(a, HD, 1)
            turn = (tabs[0], -tabs[1], -tabs[2])
            att = jnp.where(low_lane, t0, swap(t1))
            dq = rotate(jnp.where(low_lane, swap(t0), t1), *turn)
            dk = rotate(jnp.where(low_lane, t2, swap(t3)), *turn)
            dv = jnp.where(low_lane, swap(t2), t3)
            for j, part in enumerate((dq, dk, dv, att)):
                ref[:, 256 * j + 128 * e : 256 * j + 128 * e + 128] = part.astype(BF)

    gather_heads(1 - core, lf_o)
    sib[4] = remote(lf_o, lf_b.at[1], sib_s.at[4], sib_r.at[4], me.sib)
    sib[4].start()
    gather_heads(core, lf_b.at[0])

    def late(i, _):
        cols = pl.ds(pl.multiple_of(i * 256, 256), 256)
        part, grad = branch[:, cols], gnp[:, cols]
        for ref, half in ((lf_b.at[0], core), (lf_o, 1 - core)):
            at = pl.multiple_of(half * 256, 256)
            part = part + dot(ref[:, 768:1024], wout[pl.ds(at, 256), cols])
            for j in range(3):
                grad = grad + dot_nt(ref[:, 256 * j : 256 * j + 256], wqkv[j, cols, pl.ds(at, 256)])
        tps[0, :, cols] = part.astype(BF)
        tps[1, :, cols] = grad.astype(BF)
        vs[0, 0:1, cols] = jnp.sum(grad * xhat[:, cols], axis=0, keepdims=True)
        vs[0, 1:2, cols] = jnp.sum(grad, axis=0, keepdims=True)
        return 0

    lax.fori_loop(0, 4, late, 0)
    tp_copy = [remote(tps.at[i], tpl.at[i], tp_s.at[i], tp_r.at[i], me.other_tp) for i in range(2)]
    for copy in tp_copy:
        copy.start()

    v_to = (me.sib, me.x_one, me.x_three, me.z_one, me.z_three, me.y, me.other_tp)

    def v_copy(i):
        return remote(vs.at[i], vw.at[i], v_s.at[i], v_r.at[i], v_to[i])

    def v_step(i):
        v_copy(i).wait_recv()
        total = vs[i] + vw[i]
        if i == 6:
            keep = lax.broadcasted_iota(jnp.int32, (8, D), 0) < 2
            out_s[...] = jnp.where(keep, total, vs[i])
        else:
            vs[i + 1] = total
            v_copy(i + 1).start()

    v_copy(0).start()

    sib[4].wait_recv()

    def last_outer(i, _):
        rows = pl.ds(pl.multiple_of(i * 128, 128), 128)
        a0, a1 = nrm_t[rows, 0:T], nrm_t[rows, T : 2 * T]
        c0, c1 = cot_t[rows, 0:T], cot_t[rows, T : 2 * T]
        g2[0, rows, :] = (dot(a0, lf_b[0, :, 0:512]) + dot(a1, lf_b[1, :, 0:512])).astype(BF)
        g2[1, rows, 0:256] = (dot(a0, lf_b[0, :, 512:768]) + dot(a1, lf_b[1, :, 512:768])).astype(BF)
        g2[1, rows, 256:512] = (dot(c0, lf_b[0, :, 768:1024]) + dot(c1, lf_b[1, :, 768:1024])).astype(BF)
        return 0

    lax.fori_loop(0, 8, last_outer, 0)
    rs_start(2)
    v_step(0)
    ag_step(0, 2)
    ag_step(1, 2)
    v_step(1)
    rs_step(2, 0)
    v_step(2)
    ag_step(0, 1)
    ag_step(1, 1)
    rs_step(2, 1)
    v_step(3)
    rs_step(2, 2)
    v_step(4)

    tp_copy[0].wait_recv()
    tp_copy[1].wait_recv()

    def finish(i, _):
        rows = pl.ds(pl.multiple_of(i * 32, 32), 32)
        branches = tps[0, rows, :].astype(F32) + tpl[0, rows, :].astype(F32)
        out_b[rows, :] = (tok[rows, :].astype(F32) + branches.astype(BF).astype(F32) + foutb[...]).astype(BF)
        grad = (tps[1, rows, :].astype(F32) + tpl[1, rows, :].astype(F32)).astype(BF).astype(F32)
        scaled = grad * gain[...]
        x = xhat[rows, :]
        mean_one = jnp.mean(scaled, axis=-1, keepdims=True)
        mean_two = jnp.mean(scaled * x, axis=-1, keepdims=True)
        inv_std = inv[rows, 0:1]
        out_t[rows, :] = cot[0, rows, :].astype(F32) + inv_std * (scaled - mean_one - x * mean_two)
        return 0

    lax.fori_loop(0, T // 32, finish, 0)
    rs_step(2, 3)
    v_step(5)
    rs_step(2, 4)
    v_step(6)
    ag_step(0, 0)
    ag_step(1, 0)
    for s in range(4, -1, -1):
        ag_step(2, s)

    for m in range(3):
        for h in range(2):
            for s in range(2):
                fw_copy(m, h, s).wait()
                st_copy(m, h, s).wait()
            for s in range(5):
                rs_copy(m, h, s).wait_send()
                ag_copy(m, h, s).wait_send()
    for copy in sib + place_out + first_out + second_out + tp_copy:
        copy.wait_send()
    for i in range(7):
        v_copy(i).wait_send()


def call_layer(*args):
    anyspace = pl.BlockSpec(memory_space=pl.ANY)
    vmem = pl.BlockSpec(memory_space=pltpu.VMEM)
    smem = pl.BlockSpec(memory_space=pltpu.SMEM)
    dma = lambda *shape: pltpu.SemaphoreType.DMA(shape)
    V = pltpu.VMEM
    return pl.pallas_call(
        layer_kernel,
        name="layer",
        out_shape=(
            jax.ShapeDtypeStruct((T, D), BF),
            jax.ShapeDtypeStruct((T, D), F32),
            jax.ShapeDtypeStruct((8, D), F32),
            jax.ShapeDtypeStruct((3, 2, 2, 1024, 512), BF),
        ),
        in_specs=[smem, anyspace, anyspace, vmem, vmem, anyspace, anyspace, anyspace, vmem, anyspace, vmem],
        out_specs=(vmem, vmem, vmem, anyspace),
        scratch_shapes=[
            V((T, D), BF), V((2, T, D), BF), V((2, T, D), BF), V((T, D), F32), V((T, 128), F32),
            V((3, D, L), BF), V((L, D), BF), V((D, F), BF), V((F, D), BF), V((3, T, 128), F32),
            V((8, T, 256), BF), V((8, T, 256), BF), V((8, 128), jnp.int32), V((8, 8, 128), jnp.int32),
            pltpu.SMEM((8, 8, 128), jnp.int32),
            V((8 * T, 128), BF), V((8 * T, 128), BF), V((128, 8 * T), BF),
            V((8 * T, T), F32), V((8 * T, T), BF), V((8 * T, 128), F32), V((8, T, 256), BF),
            V((8, T, 256), BF), V((8, T, 256), BF),
            V((T, 1024), BF), V((2, T, 1024), BF), V((T, 1024), BF), V((2, T, 1024), BF),
            V((T, 1024), BF), V((2, T, 1024), BF),
            V((D, 2 * T), BF), V((D, 2 * T), BF), V((1024, 2 * T), BF),
            V((T, D), F32), V((T, D), F32), V((2, T, D), BF), V((2, T, D), BF),
            V((2, 1024, 512), BF), V((2, 1024, 512), BF), V((2, 1024, 512), BF),
            V((2, 992, 512), BF), V((2, 992, 512), BF), V((2, 992, 512), BF),
            V((2, 1024, 512), BF), V((2, 1024, 512), BF), V((2, 1024, 512), BF),
            V((7, 8, D), F32), V((7, 8, D), F32),
            dma(6), dma(5), dma(5), dma(7), dma(7), dma(7), dma(7), dma(7), dma(7), dma(2), dma(2),
            dma(3, 2, 5), dma(3, 2, 5), dma(3, 2, 5), dma(3, 2, 5),
            dma(3, 2, 2), dma(3, 2, 2), dma(3, 2, 2), dma(7), dma(7), pltpu.SemaphoreType.DMA(()),
        ],
        compiler_params=pltpu.CompilerParams(
            collective_id=0, has_side_effects=True, vmem_limit_bytes=62 * 2**20
        ),
    )(*args)


def widen_kernel(a, b, c, d, fc_out, fc_in, qkv, out):
    for half in range(2):
        fc_out[:, 512 * half : 512 * half + 512] = a[0, 0, half].astype(F32)
    for core in range(2):
        for half in range(2):
            start = 1024 * core + 512 * half
            fc_in[:, start : start + 512] = b[0, core, half].astype(F32)
        here = slice(256 * core, 256 * core + 256)
        qkv[0, :, here] = c[0, core, 0, :, 0:256].astype(F32)
        qkv[1, :, here] = c[0, core, 0, :, 256:512].astype(F32)
        qkv[2, :, here] = c[0, core, 1, :, 0:256].astype(F32)
    out[...] = d[0, 0, 0].astype(F32).T


def call_widen(grads):
    n = 8
    spec = pl.BlockSpec
    return pl.pallas_call(
        widen_kernel,
        name="widen",
        grid=(n,),
        in_specs=[
            spec((1, 1, 2, 2048 // n, 512), lambda i: (0, i // (n // 2), 0, i % (n // 2), 0)),
            spec((1, 2, 2, 1024 // n, 512), lambda i: (1, 0, 0, i, 0)),
            spec((1, 2, 2, 1024 // n, 512), lambda i: (2, 0, 0, i, 0)),
            spec((1, 1, 1, 1024, 128), lambda i: (2, i // 4, 1, 0, 2 + i // 2 % 2)),
        ],
        out_specs=(
            spec((2048 // n, 1024), lambda i: (i, 0)),
            spec((1024 // n, 2048), lambda i: (i, 0)),
            spec((3, 1024 // n, 512), lambda i: (0, i, 0)),
            spec((128, 1024), lambda i: (i // 2, 0)),
        ),
        out_shape=(
            jax.ShapeDtypeStruct((F, D), F32),
            jax.ShapeDtypeStruct((D, F), F32),
            jax.ShapeDtypeStruct((3, D, L), F32),
            jax.ShapeDtypeStruct((L, D), F32),
        ),
        compiler_params=pltpu.CompilerParams(vmem_limit_bytes=60 * 2**20),
    )(grads, grads, grads, grads)


def local(
    tokens, positions, cotangent, ln_gain, ln_bias, qkv_weight, out_weight,
    fc_in_weight, fc_in_bias, fc_out_weight, fc_out_bias,
):
    block_out, tokens_grad, small, grads = call_layer(
        positions,
        tokens[0],
        cotangent[0],
        ln_gain[None],
        ln_bias[None],
        qkv_weight.transpose(1, 0, 2),
        out_weight,
        fc_in_weight,
        fc_in_bias[None],
        fc_out_weight,
        fc_out_bias[None],
    )
    fc_out_grad, fc_in_grad, qkv_grad, out_grad = call_widen(grads)
    return (
        block_out[None],
        tokens_grad[None],
        small[0],
        small[1],
        qkv_grad.transpose(1, 0, 2),
        out_grad,
        fc_in_grad,
        small[2:4].reshape(F),
        fc_out_grad,
        small[4],
    )


def solution(mesh):
    placed = (
        P("seq", "ctx", None), P("seq", "ctx"), P("seq", "ctx", None), P(), P(),
        P(None, None, "tp"), P("tp", None), P(None, "tp"), P("tp"), P("tp", None), P(),
    )
    return jax.shard_map(
        local,
        mesh=mesh,
        in_specs=placed,
        out_specs=(
            P("seq", "ctx", None), P("seq", "ctx", None), P(), P(), P(None, None, "tp"),
            P("tp", None), P(None, "tp"), P("tp"), P("tp", None), P(),
        ),
        check_vma=False,
    )
```

```python
import math
from types import SimpleNamespace

import jax
import jax.numpy as jnp
from jax import lax
from jax.experimental import pallas as pl
from jax.experimental.pallas import tpu as pltpu
from jax.sharding import PartitionSpec as P

HD = 64
ROT = 32
T = 256
D = 1024
L = 512
F = 2048
MESH = pl.DeviceIdType.MESH
BF = jnp.bfloat16
F32 = jnp.float32
EPS = 1e-05
ROWS = (1024, 1024, 1024, 512)
WIDE = (512, 512, 384, 256)
ORDER = ("xz", "xz", "xz", "xz")


def dot(a, b):
    return lax.dot_general(a, b, (((1,), (0,)), ((), ())), preferred_element_type=F32)


def dot_nt(a, b):
    return lax.dot_general(a, b, (((1,), (1,)), ((), ())), preferred_element_type=F32)


def xor(a, b):
    return a + b - 2 * a * b


class Place:
    def __init__(self):
        seq, ctx, tp = lax.axis_index("seq"), lax.axis_index("ctx"), lax.axis_index("tp")
        self.seq, self.ctx, self.tp = seq, ctx, tp
        self.z, self.core, self.x, self.yh = seq // 2, seq % 2, ctx // 2, ctx % 2
        c, x, z = self.core, self.x, self.z
        flip = lambda i: i + 1 - 2 * (i % 2)
        self.sib = (z * 2 + 1 - c, ctx, tp)
        self.other_tp = (seq, ctx, 1 - tp)
        self.y = (seq, x * 2 + 1 - self.yh, tp)
        self.x_one = (seq, flip(x) * 2 + self.yh, tp)
        self.x_three = (seq, (3 - x) * 2 + self.yh, tp)
        self.z_one = (flip(z) * 2 + c, ctx, tp)
        self.z_three = ((3 - z) * 2 + c, ctx, tp)
        c = {"xz": c, "z": 1, "x": 0}
        self.order = [Order(self, c[kind]) for kind in ORDER]


class Order:
    def __init__(self, me, c):
        x, z = me.x, me.z
        pick = lambda a, b: tuple((1 - c) * p + c * q for p, q in zip(a, b))
        u, v = (1 - c) * x + c * z, (1 - c) * z + c * x
        one, three = pick(me.x_one, me.z_one), pick(me.x_three, me.z_three)
        self.before, self.after = (one, three), (three, one)
        u0, u1 = u % 2, u // 2
        w0 = 1 - u0
        self.keep = (2 * xor(u0, u1) + u1, 2 * u1 + u0)
        self.give = (2 * xor(u0, u1) + 1 - u1, 2 * u1 + 1 - u0)
        self.their_give = (2 * xor(w0, u1) + 1 - u1, 2 * (1 - u1) + u0)
        self.their_keep = (2 * xor(w0, u1) + u1, 2 * (1 - u1) + 1 - u0)
        self.place = v * 2 + me.yh
        self.others = []
        for k in range(1, 8):
            to = lax.rem(self.place + k, 8)
            there = to // 2
            zz, xx = (1 - c) * there + c * z, (1 - c) * x + c * there
            self.others.append((to, (zz * 2 + me.core, xx * 2 + to % 2, me.tp)))


def remote(src, dst, send, recv, device):
    return pltpu.make_async_remote_copy(
        src_ref=src, dst_ref=dst, send_sem=send, recv_sem=recv, device_id=device, device_id_type=MESH
    )


def rotate(u, cosine, even, odd):
    return u * cosine + pltpu.roll(u, 127, 1) * even + pltpu.roll(u, 1, 1) * odd


def keys(j):
    return slice(j * T, j * T + T)


def tri(r):
    return r * (r + 1) // 2 * T


def layer_kernel(
    pos_h, tok_h, cot_h, gain, lnb, wqkv_h, wout_h, fin_h, finb, fout_h, foutb,
    out_b, out_t, out_s, out_0, out_1, out_2, out_3,
    pos, tok, cot, nrm, xhat, inv, wqkv, wout, fin, fout, tabs, send1, land1, ptile, pland, psm, qg, kv,
    kvt, sbuf, pbuf, atts, aq, send2, land2, sib_att, send3, land3, act_o, act_b, gh_o, gh_b, lf_o, lf_b,
    nrm_t, tps, tpl, g0, g1, g2, g3, l0, l1, l2, l3, r0, r1, r2, r3, t0, t1, t2, t3, w0, w1, w2, w3, vs,
    vw, blk, tgr, in_sem, sib_s, sib_r, all_s, all_r, tp_s, tp_r, rs_s, rs_r, fw_s, fw_r, st_s, v_s, v_r,
    o_s,
):
    me = Place()
    core, ctx = me.core, me.ctx
    g, lands, res, outs = (g0, g1, g2, g3), (l0, l1, l2, l3), (r0, r1, r2, r3), (out_0, out_1, out_2, out_3)
    slots, whole_q = (t0, t1, t2, t3), (w0, w1, w2, w3)

    loads = [
        pltpu.make_async_copy(a, b, in_sem.at[i])
        for i, (a, b) in enumerate(
            (
                (pos_h, pos), (tok_h, tok), (cot_h, cot.at[0]), (wqkv_h, wqkv), (wout_h, wout),
                (fin_h, fin), (fout_h, fout),
            )
        )
    ]
    for copy in loads:
        copy.start()

    barrier = pltpu.get_barrier_semaphore()
    peers = [(me.seq, lax.rem(ctx + k, 8), me.tp) for k in range(1, 8)]
    across = [
        ((lax.rem(me.z + k, 4) * 2 + core, me.x * 2 + yh, me.tp)) for k in range(1, 4) for yh in range(2)
    ]
    for device in peers + across + [me.sib, me.other_tp]:
        pl.semaphore_signal(barrier, inc=1, device_id=device, device_id_type=MESH)

    loads[0].wait()
    first = pos[0, 0]
    lane = lax.broadcasted_iota(jnp.int32, (T, 128), 1)
    row = lax.broadcasted_iota(jnp.int32, (T, 128), 0)
    in_head = lane % HD
    low_lane = lane < HD
    freq = jnp.exp((in_head // 2).astype(F32) * (-2.0 * math.log(10000.0) / ROT))
    theta = (row + first).astype(F32) * freq
    turning = in_head < ROT
    sine = jnp.where(turning, jnp.sin(theta), 0.0)
    tabs[0] = jnp.where(turning, jnp.cos(theta), 1.0)
    tabs[1] = jnp.where(lane % 2 == 0, -sine, 0.0)
    tabs[2] = jnp.where(lane % 2 == 0, 0.0, sine)
    ptile[...] = jnp.full((8, 128), first, jnp.int32)

    loads[1].wait()

    def norm_rows(i, _):
        rows = pl.ds(pl.multiple_of(i * 64, 64), 64)
        x = tok[rows, :].astype(F32)
        x = x - jnp.mean(x, axis=-1, keepdims=True)
        inv_std = lax.rsqrt(jnp.mean(x * x, axis=-1, keepdims=True) + EPS)
        x = x * inv_std
        xhat[rows, :] = x
        inv[rows, :] = jnp.broadcast_to(inv_std, (64, 128))
        nrm[0, rows, :] = (x * gain[...] + lnb[...]).astype(BF)
        return 0

    lax.fori_loop(0, T // 64, norm_rows, 0)

    loads[2].wait()
    pl.semaphore_wait(barrier, 15)

    sib_pairs = (
        (cot.at[0], cot.at[1]),
        (nrm.at[0], nrm.at[1]),
        (act_o, act_b.at[1]),
        (gh_o, gh_b.at[1]),
        (land2.at[pl.ds(4 * (1 - core), 4)], sib_att),
        (lf_o, lf_b.at[1]),
    )

    def to_sib(i):
        return remote(*sib_pairs[i], sib_s.at[i], sib_r.at[i], me.sib)

    def to_all(src, dst, i):
        for k in range(1, 8):
            to = lax.rem(ctx + k, 8)
            here = src if i == 0 else src.at[to]
            remote(here, dst.at[ctx], all_s.at[i], all_r.at[i], peers[k - 1]).start()
        dst[ctx] = src[...] if i == 0 else src[ctx]

    def all_seven(dst, i):
        return remote(dst.at[pl.ds(0, 7)], dst.at[pl.ds(0, 7)], all_s.at[i], all_r.at[i], me.sib)

    to_sib(0).start()
    to_sib(1).start()

    loads[3].wait()
    loads[4].wait()
    to_all(ptile, pland, 0)
    normed = nrm[0]
    swap = lambda a: pltpu.roll(a, HD, 1)
    for e in range(4):
        cols = slice(128 * e, 128 * e + 128)
        turn = (tabs[0], tabs[1], tabs[2])
        q = rotate(dot(normed, wqkv[0, :, cols]), *turn) * HD ** (-0.5)
        k = rotate(dot(normed, wqkv[1, :, cols]), *turn)
        v = dot(normed, wqkv[2, :, cols])
        ga = dot_nt(cot[0], wout[cols, :])
        send1[2 * e, :, 0:128] = jnp.where(low_lane, q, swap(ga)).astype(BF)
        send1[2 * e, :, 128:256] = jnp.where(low_lane, k, swap(v)).astype(BF)
        send1[2 * e + 1, :, 0:128] = jnp.where(low_lane, swap(q), ga).astype(BF)
        send1[2 * e + 1, :, 128:256] = jnp.where(low_lane, swap(k), v).astype(BF)
    to_all(send1, land1, 1)

    loads[5].wait()
    loads[6].wait()
    vs[0] = jnp.zeros((8, D), F32)

    def hidden(half, act_ref, gh_ref, i):
        start = pl.multiple_of(half * 1024 + i * 256, 256)
        here = pl.ds(pl.multiple_of(i * 256, 256), 256)
        u = dot(nrm[0], fin[:, pl.ds(start, 256)]) + finb[:, pl.ds(start, 256)]
        z = math.sqrt(2.0 / math.pi) * (u + 0.044715 * u * u * u)
        t = jnp.tanh(z)
        act_ref[:, here] = (0.5 * u * (1.0 + t)).astype(BF)
        slope = 0.5 * (1.0 + t) + (0.5 * math.sqrt(2.0 / math.pi)) * u * (1.0 - t * t) * (
            1.0 + 3 * 0.044715 * u * u
        )
        grad = dot_nt(cot[0], fout[pl.ds(start, 256), :]) * slope
        low = grad.astype(BF)
        gh_ref[:, here] = low
        vs[0, pl.ds(2 + half, 1), here] = jnp.sum(low.astype(F32), axis=0, keepdims=True)

    def other_half(i, _):
        hidden(1 - core, act_o, gh_o, i)
        return 0

    def own_half(i, _):
        hidden(core, act_b.at[0], gh_b.at[0], i)
        return 0

    lax.fori_loop(0, 4, other_half, 0)
    to_sib(2).start()
    to_sib(3).start()
    lax.fori_loop(0, 4, own_half, 0)

    def turn_over(src, dst):
        def body(i, _):
            here = pl.ds(pl.multiple_of(i * 128, 128), 128)
            for token in range(2):
                dst[token, here, :] = src[token, :, here].T
            return 0

        lax.fori_loop(0, D // 128, body, 0)

    def quarter(m, q):
        return pl.ds(pl.multiple_of(q * (ROWS[m] // 4), ROWS[m] // 4), ROWS[m] // 4)

    def swap_copy(m, h, k):
        o = me.order[m]
        q = (o.their_give, o.their_keep, o.give)[k][h]
        device = o.after[h] if k == 2 else o.before[h]
        return remote(g[m].at[h, quarter(m, q)], lands[m].at[k, h], rs_s.at[m, 0], rs_r.at[m, min(k, 1)], device)

    def arrived(m, ref, i):
        remote(ref, ref, rs_s.at[m, 0], rs_r.at[m, i], me.sib).wait_recv()

    def add(m, h, into, rows, start, *terms):
        block = 64

        def body(i, _):
            here = pl.ds(pl.multiple_of(i * block, block), block)
            total = g[m][h, pl.ds(pl.multiple_of(start + i * block, block), block), :].astype(F32)
            for k in terms:
                total = total + lands[m][k, h, here, :].astype(F32)
            if into is None:
                g[m][h, pl.ds(pl.multiple_of(start + i * block, block), block), :] = total.astype(BF)
            else:
                lands[m][into, h, here, :] = total.astype(BF)
            return 0

        lax.fori_loop(0, rows // block, body, 0)

    def first_sum(m):
        arrived(m, lands[m].at[0], 0)
        for h in range(2):
            add(m, h, None, ROWS[m] // 4, me.order[m].give[h] * (ROWS[m] // 4), 0)
            swap_copy(m, h, 2).start()

    def second_sum(m):
        arrived(m, lands[m].at[pl.ds(1, 2)], 1)
        for h in range(2):
            add(m, h, 2, ROWS[m] // 4, me.order[m].keep[h] * (ROWS[m] // 4), 1, 2)
        o, n = me.order[m], ROWS[m] // 32
        for to, device in o.others:
            piece = lands[m].at[2, :, pl.ds(pl.multiple_of(to * n, n), n)]
            remote(piece, slots[m].at[o.place], rs_s.at[m, 1], rs_r.at[m, 2], device).start()

    def third_sum(m):
        seven = slots[m].at[pl.ds(0, 7)]
        arrived(m, seven, 2)
        o, n = me.order[m], ROWS[m] // 32
        here = pl.ds(pl.multiple_of(o.place * n, n), n)
        slots[m][o.place] = lands[m][2, :, here, :]
        for h in range(2):
            total = slots[m][0, h].astype(F32)
            for k in range(1, 8):
                total = total + slots[m][k, h].astype(F32)
            whole_q[m][h, here, :] = total.astype(BF)
        piece = whole_q[m].at[:, here]
        for to, device in o.others:
            remote(piece, piece, rs_s.at[m, 2], rs_r.at[m, 3], device).start()

    def hand_over(m, h, src, q):
        there = outs[m].at[core, h, quarter(m, q)]
        remote(src, there, fw_s.at[m], fw_r.at[m], me.sib).start()
        pltpu.make_async_copy(src, there, st_s.at[m]).start()

    def spread(m, h, src, q, k):
        o = me.order[m]
        device = (o.before if k else o.after)[h]
        remote(src, res[m].at[h, quarter(m, q)], rs_s.at[m, 3], rs_r.at[m, 4 + k], device).start()

    def first_gather(m):
        arrived(m, slots[m].at[pl.ds(0, 7)], 3)
        o = me.order[m]
        for k in range(2):
            for h in range(2):
                spread(m, h, whole_q[m].at[h], o.keep[h], k)
        for h in range(2):
            hand_over(m, h, whole_q[m].at[h], o.keep[h])

    def second_gather(m):
        arrived(m, lands[m].at[0], 4)
        o = me.order[m]
        for h in range(2):
            src = res[m].at[h, quarter(m, o.give[h])]
            spread(m, h, src, o.give[h], 1)
            hand_over(m, h, src, o.give[h])

    def third_gather(m):
        arrived(m, lands[m].at[pl.ds(0, 2)], 5)
        o = me.order[m]
        for h in range(2):
            for q in (o.their_give[h], o.their_keep[h]):
                hand_over(m, h, res[m].at[h, quarter(m, q)], q)

    def outer(m, left_t, right):
        o = me.order[m]
        for k, qs in enumerate((o.their_give, o.their_keep, o.give, o.keep)):
            for h in range(2):
                rows = quarter(m, qs[h])
                cols = slice(WIDE[m] * h, WIDE[m] * h + WIDE[m])
                total = dot(left_t[0, rows, :], right[0, :, cols]) + dot(left_t[1, rows, :], right[1, :, cols])
                g[m][h, rows, :] = total.astype(BF)
                if k < 2:
                    swap_copy(m, h, k).start()

    act_t = pbuf.at[pl.ds(0, 2 * D)].reshape(2, D, T)
    to_sib(2).wait_recv()
    turn_over(act_b, act_t)
    to_sib(0).wait_recv()
    outer(0, act_t, cot)
    to_sib(1).wait_recv()
    turn_over(nrm, nrm_t)
    to_sib(3).wait_recv()
    outer(1, nrm_t, gh_b)
    vs[0, 4:5, :] = jnp.sum(cot[0].astype(F32), axis=0, keepdims=True)

    all_seven(pland, 0).wait_recv()
    to_scalar = pltpu.make_async_copy(pland, psm, o_s.at[2])
    to_scalar.start()
    all_seven(land1, 1).wait_recv()
    to_scalar.wait()
    rank = [psm[c, 0, 0] // T for c in range(8)]
    for r in range(8):
        at = 0
        for c in range(8):
            at = jnp.where(rank[c] == r, c, at)
        block = land1[at]
        qg[keys(r), :] = block[:, 0:128]
        kv[keys(r), :] = block[:, 128:256]
        kvt[:, keys(r)] = block[:, 128:256].T

    causal = lax.broadcasted_iota(jnp.int32, (T, T), 0) <= lax.broadcasted_iota(jnp.int32, (T, T), 1)
    deltas = [None] * 8

    def split(r):
        both_lanes = qg[keys(r), :]
        zero = jnp.zeros_like(both_lanes)
        return jnp.where(low_lane, both_lanes, zero), jnp.where(low_lane, zero, both_lanes)

    def scores(r):
        q, _ = split(r)
        top = jnp.full((8, T), -1e30, F32)
        for j in range(r + 1):
            s = dot_nt(kv[keys(j), :], q)
            if j == r:
                s = jnp.where(causal, s, -1e30)
            sbuf[r % 2, keys(j), :] = s
            top = jnp.maximum(top, jnp.max(s.reshape(T // 8, 8, T), axis=0))
        return top

    def weigh(r, top):
        top = jnp.max(top, axis=0, keepdims=True)
        total, att = jnp.zeros((8, T), F32), jnp.zeros((HD, T), F32)
        for j in range(r + 1):
            e = jnp.exp(sbuf[r % 2, keys(j), :] - top)
            total = total + jnp.sum(e.reshape(T // 8, 8, T), axis=0)
            low = e.astype(BF)
            pbuf[tri(r) + j * T : tri(r) + j * T + T, :] = low
            att = att + dot(kvt[HD:, keys(j)], low)
        scale = 1.0 / jnp.sum(total, axis=0, keepdims=True)
        att = att * scale
        atts[r] = att.astype(BF)
        both_lanes = qg[keys(r), :]
        ga_t = (both_lanes.T.astype(F32)[HD:, :] * scale).astype(BF)
        deltas[r] = jnp.sum(ga_t.astype(F32) * att, axis=0, keepdims=True)
        ga = jnp.concatenate([jnp.zeros((HD, T), BF), ga_t], axis=0).T
        qg[keys(r), :] = jnp.where(low_lane, both_lanes, ga)

    def back(r):
        q, ga = split(r)
        dq = jnp.zeros((HD, T), F32)
        for j in range(r + 1):
            prob = pbuf[tri(r) + j * T : tri(r) + j * T + T, :]
            dp = dot_nt(kv[keys(j), :], ga)
            ds = (prob.astype(F32) * (dp - deltas[r])).astype(BF)
            update = dot(ds, q) + dot(prob, ga)
            if r == 7:
                sbuf[0, keys(j), 0:128] = update
            else:
                sbuf[0, keys(j), 0:128] += update
            dq = dq + dot(kvt[:HD, keys(j)], ds)
        dq = (dq * HD ** (-0.5)).astype(BF)
        aq[r, 0:256, :] = sbuf[0, keys(r), 0:128].astype(BF)
        aq[r, 256:320, :] = dq[:, 0:128]
        aq[r, 320:384, :] = dq[:, 128:256]

    ahead = scores(7)
    for r in range(7, -1, -1):
        now = ahead
        if r:
            ahead = scores(r - 1)
        weigh(r, now)
    for c in range(8):
        send2[c] = atts[rank[c]]
    to_all(send2, land2, 2)
    back(7)
    back(6)
    back(5)
    first_sum(0)
    back(4)
    back(3)
    first_sum(1)
    back(2)
    back(1)
    back(0)
    for c in range(8):
        send3[c] = aq[rank[c]]
    to_all(send3, land3, 3)

    own, oth = pl.multiple_of(core * 1024, 1024), pl.multiple_of((1 - core) * 1024, 1024)
    all_seven(land2, 2).wait_recv()
    to_sib(4).start()
    att_rows = land2[...].reshape(L, T).T

    def branch(i, _):
        cols = pl.ds(pl.multiple_of(i * 256, 256), 256)
        part = dot(act_b[0], fout[pl.ds(own, 1024), cols]) + dot(act_o[...], fout[pl.ds(oth, 1024), cols])
        tps[0, i] = (part + dot(att_rows, wout[:, cols])).astype(BF)
        return 0

    lax.fori_loop(0, 4, branch, 0)

    def tp_copy(i, j):
        return remote(tps.at[i, j], tpl.at[i, j], tp_s.at[i], tp_r.at[i], me.other_tp)

    def tp_start(*which):
        for i, j in which:
            tp_copy(i, j).start()

    tp_start((0, 0), (0, 1), (0, 2), (0, 3))
    to_sib(4).wait_recv()
    mine = land2[pl.ds(4 * core, 4)].reshape(T, T)
    theirs = sib_att[...].reshape(T, T)
    for h in range(2):
        for q in range(2):
            cols = slice(512 * h + 256 * q, 512 * h + 256 * q + 256)
            g3[h, 256 * q : 256 * q + 256, :] = (dot(mine, cot[0, :, cols]) + dot(theirs, cot[1, :, cols])).astype(BF)
    for k in range(2):
        for h in range(2):
            swap_copy(3, h, k).start()

    def mixed(i, _):
        cols = pl.ds(pl.multiple_of(i * 256, 256), 256)
        sbuf[1, cols, :] = dot_nt(gh_b[0], fin[cols, pl.ds(own, 1024)]) + dot_nt(gh_o[...], fin[cols, pl.ds(oth, 1024)])
        return 0

    lax.fori_loop(0, 4, mixed, 0)
    second_sum(0)
    second_sum(1)
    third_sum(0)
    all_seven(land3, 3).wait_recv()

    def gather_heads(half, ref):
        for e in range(2):
            low, high = 4 * half + 2 * e, 4 * half + 2 * e + 1
            t0, t1 = land3[low, 0:256, :].astype(F32), land3[high, 0:256, :].astype(F32)
            dq_t = jnp.concatenate(
                [
                    jnp.concatenate([land3[i, 256:320, :], land3[i, 320:384, :]], axis=1)
                    for i in (low, high)
                ],
                axis=0,
            )
            turn = (tabs[0], -tabs[1], -tabs[2])
            dq = rotate(dq_t.T.astype(F32), *turn)
            dk = rotate(jnp.where(low_lane, t0, swap(t1)), *turn)
            dv = jnp.where(low_lane, swap(t0), t1)
            for j, part in enumerate((dq, dk, dv)):
                ref[:, 256 * j + 128 * e : 256 * j + 128 * e + 128] = part.astype(BF)

    gather_heads(1 - core, lf_o)
    to_sib(5).start()
    gather_heads(core, lf_b.at[0])
    third_sum(1)
    to_sib(5).wait_recv()
    outer(2, nrm_t, lf_b)

    def late(i, _):
        cols = pl.ds(pl.multiple_of(i * 256, 256), 256)
        grad = sbuf[1, cols, :]
        for ref, half in ((lf_b.at[0], core), (lf_o, 1 - core)):
            at = pl.multiple_of(half * 256, 256)
            for j in range(3):
                grad = grad + dot_nt(ref[:, 256 * j : 256 * j + 256], wqkv[j, cols, pl.ds(at, 256)])
        tps[1, i] = grad.astype(BF)
        vs[0, 0:1, cols] = jnp.sum(grad * xhat[:, cols], axis=0, keepdims=True)
        vs[0, 1:2, cols] = jnp.sum(grad, axis=0, keepdims=True)
        return 0

    lax.fori_loop(0, 4, late, 0)

    v_to = (me.sib, me.y, me.x_one, me.x_three, me.z_one, me.z_three, me.other_tp)

    def v_copy(i):
        return remote(vs.at[i], vw.at[i], v_s.at[0], v_r.at[i], v_to[i])

    def v_step(i):
        v_copy(i).wait_recv()
        total = vs[i] + vw[i]
        if i == 6:
            here = lax.broadcasted_iota(jnp.int32, (8, D), 0) < 2
            out_s[...] = jnp.where(here, total, vs[i])
        else:
            vs[i + 1] = total
            v_copy(i + 1).start()

    v_copy(0).start()

    def finish(i, _):
        rows = pl.ds(pl.multiple_of(i * 32, 32), 32)

        def whole(k):
            parts = [tps[k, j, rows, :].astype(F32) + tpl[k, j, rows, :].astype(F32) for j in range(4)]
            return jnp.concatenate(parts, axis=1).astype(BF).astype(F32)

        blk[rows, :] = (tok[rows, :].astype(F32) + whole(0) + foutb[...]).astype(BF)
        grad = whole(1)
        scaled = grad * gain[...]
        x = xhat[rows, :]
        mean_one = jnp.mean(scaled, axis=-1, keepdims=True)
        mean_two = jnp.mean(scaled * x, axis=-1, keepdims=True)
        inv_std = inv[rows, 0:1]
        tgr[rows, :] = cot[0, rows, :].astype(F32) + inv_std * (scaled - mean_one - x * mean_two)
        return 0

    to_out = [pltpu.make_async_copy(blk, out_b, o_s.at[0]), pltpu.make_async_copy(tgr, out_t, o_s.at[1])]

    def tp_all(i):
        return remote(tps.at[i], tpl.at[i], tp_s.at[i], tp_r.at[i], me.other_tp)

    first_sum(2)
    tp_start((1, 0), (1, 1))
    first_sum(3)
    first_gather(0)
    first_gather(1)
    second_sum(2)
    v_step(0)
    v_step(1)
    second_sum(3)
    third_sum(2)
    third_sum(3)
    first_gather(2)
    v_step(2)
    v_step(3)
    first_gather(3)
    second_gather(0)
    second_gather(1)
    tp_start((1, 2), (1, 3))
    v_step(4)
    second_gather(2)
    second_gather(3)
    v_step(5)
    third_gather(0)
    third_gather(1)
    v_step(6)
    tp_all(0).wait_recv()
    tp_all(1).wait_recv()
    lax.fori_loop(0, T // 32, finish, 0)
    to_out[0].start()
    to_out[1].start()
    third_gather(3)
    third_gather(2)
    for m in range(4):
        seven = slots[m].at[pl.ds(0, 7)]
        for i, ref in enumerate((lands[m], seven, seven, lands[m])):
            remote(ref, ref, rs_s.at[m, i], rs_r.at[m, 0], me.sib).wait_send()
        half_out = outs[m].at[1 - core]
        remote(res[m], half_out, fw_s.at[m], fw_r.at[m], me.sib).wait()
        pltpu.make_async_copy(res[m], outs[m].at[core], st_s.at[m]).wait()
    for i in range(6):
        to_sib(i).wait_send()
    all_seven(pland, 0).wait_send()
    all_seven(land1, 1).wait_send()
    all_seven(land2, 2).wait_send()
    all_seven(land3, 3).wait_send()
    for i in range(2):
        tp_all(i).wait_send()
        to_out[i].wait()
    remote(vs, vw, v_s.at[0], v_r.at[0], me.sib).wait_send()


def call_layer(*args):
    anyspace = pl.BlockSpec(memory_space=pl.ANY)
    vmem = pl.BlockSpec(memory_space=pltpu.VMEM)
    dma = lambda *shape: pltpu.SemaphoreType.DMA(shape)
    V = pltpu.VMEM
    return pl.pallas_call(
        layer_kernel,
        name="layer",
        out_shape=(
            jax.ShapeDtypeStruct((T, D), BF),
            jax.ShapeDtypeStruct((T, D), F32),
            jax.ShapeDtypeStruct((8, D), F32),
        )
        + tuple(jax.ShapeDtypeStruct((2, 2, ROWS[m], WIDE[m]), BF) for m in range(4)),
        in_specs=[anyspace] * 3 + [vmem, vmem, anyspace, anyspace, anyspace, vmem, anyspace, vmem],
        out_specs=(anyspace, anyspace, vmem) + (anyspace,) * 4,
        scratch_shapes=[
            pltpu.SMEM((1, T), jnp.int32), V((T, D), BF), V((2, T, D), BF), V((2, T, D), BF), V((T, D), F32),
            V((T, 128), F32), V((3, D, L), BF), V((L, D), BF), V((D, F), BF), V((F, D), BF), V((3, T, 128), F32),
            V((8, T, 256), BF), V((8, T, 256), BF), V((8, 128), jnp.int32), V((8, 8, 128), jnp.int32),
            pltpu.SMEM((8, 8, 128), jnp.int32), V((8 * T, 128), BF), V((8 * T, 128), BF), V((128, 8 * T), BF),
            V((2, 8 * T, T), F32), V((36 * T, T), BF), V((8, HD, T), BF), V((8, 384, 128), BF), V((8, HD, T), BF),
            V((8, HD, T), BF), V((4, HD, T), BF), V((8, 384, 128), BF), V((8, 384, 128), BF), V((T, 1024), BF),
            V((2, T, 1024), BF), V((T, 1024), BF), V((2, T, 1024), BF), V((T, 768), BF), V((2, T, 768), BF),
            V((2, D, T), BF), V((2, 4, T, T), BF), V((2, 4, T, T), BF), V((2, 1024, 512), BF),
            V((2, 1024, 512), BF), V((2, 1024, 384), BF), V((2, 512, 256), BF), V((3, 2, 256, 512), BF),
            V((3, 2, 256, 512), BF), V((3, 2, 256, 384), BF), V((3, 2, 128, 256), BF), V((2, 1024, 512), BF),
            V((2, 1024, 512), BF), V((2, 1024, 384), BF), V((2, 512, 256), BF), V((8, 2, 32, 512), BF),
            V((8, 2, 32, 512), BF), V((8, 2, 32, 384), BF), V((8, 2, 16, 256), BF), V((2, 256, 512), BF),
            V((2, 256, 512), BF), V((2, 256, 384), BF), V((2, 128, 256), BF), V((7, 8, D), F32), V((7, 8, D), F32),
            V((T, D), BF), V((T, D), F32), dma(7), dma(6), dma(6), dma(4), dma(4), dma(2), dma(2), dma(4, 4),
            dma(4, 6), dma(4), dma(4), dma(4), dma(1), dma(7), dma(3),
        ],
        compiler_params=pltpu.CompilerParams(
            collective_id=0, has_side_effects=True, vmem_limit_bytes=63 * 2**20
        ),
    )(*args)


def widen_kernel(
    a, b, c, d, block, grads, small,
    fc_out, fc_in, qkv, out, block_out, tokens_grad, gain, bias, fc_in_bias, fc_out_bias,
):
    for half in range(2):
        fc_out[:, 512 * half : 512 * half + 512] = a[0, half].astype(F32)
    for core in range(2):
        for half in range(2):
            start = 1024 * core + 512 * half
            fc_in[:, start : start + 512] = b[core, half].astype(F32)
        here = 256 * core
        qkv[0, :, here : here + 256] = c[core, 0, :, 0:256].astype(F32)
        qkv[1, :, here : here + 128] = c[core, 0, :, 256:384].astype(F32)
        qkv[1, :, here + 128 : here + 256] = c[core, 1, :, 0:128].astype(F32)
        qkv[2, :, here : here + 256] = c[core, 1, :, 128:384].astype(F32)
    for half in range(2):
        for part in range(2):
            start = 512 * half + 256 * part
            out[:, start : start + 256] = d[0, half, part].astype(F32)
    block_out[...] = block[...]
    tokens_grad[...] = grads[...]
    gain[...] = small[0:1, :]
    bias[...] = small[1:2, :]
    fc_in_bias[:, 0:1024] = small[2:3, :]
    fc_in_bias[:, 1024:2048] = small[3:4, :]
    fc_out_bias[...] = small[4:5, :]


def call_widen(block, grads, small, a, b, c, d):
    n = 8
    half = n // 2
    spec = pl.BlockSpec
    shape = jax.ShapeDtypeStruct
    return pl.pallas_call(
        widen_kernel,
        name="widen",
        grid=(n,),
        in_specs=[
            spec((1, 2, F // n, 512), lambda i: (i // half, 0, i % half, 0)),
            spec((2, 2, D // n, 512), lambda i: (0, 0, i, 0)),
            spec((2, 2, D // n, 384), lambda i: (0, 0, i, 0)),
            spec((1, 2, 2, L // n, 256), lambda i: (i // half, 0, 0, i % half, 0)),
            spec((T // n, D), lambda i: (i, 0)),
            spec((T // n, D), lambda i: (i, 0)),
            spec((8, D), lambda i: (0, 0)),
        ],
        out_specs=(
            spec((F // n, D), lambda i: (i, 0)),
            spec((D // n, F), lambda i: (i, 0)),
            spec((3, D // n, L), lambda i: (0, i, 0)),
            spec((L // n, D), lambda i: (i, 0)),
            spec((T // n, D), lambda i: (i, 0)),
            spec((T // n, D), lambda i: (i, 0)),
            spec((1, D), lambda i: (0, 0)),
            spec((1, D), lambda i: (0, 0)),
            spec((1, F), lambda i: (0, 0)),
            spec((1, D), lambda i: (0, 0)),
        ),
        out_shape=(
            shape((F, D), F32), shape((D, F), F32), shape((3, D, L), F32), shape((L, D), F32),
            shape((T, D), BF), shape((T, D), F32),
            shape((1, D), F32), shape((1, D), F32), shape((1, F), F32), shape((1, D), F32),
        ),
        compiler_params=pltpu.CompilerParams(vmem_limit_bytes=60 * 2**20),
    )(a, b, c, d.reshape(2, 2, 2, 256, 256), block, grads, small)


def local(
    tokens, positions, cotangent, ln_gain, ln_bias, qkv_weight, out_weight,
    fc_in_weight, fc_in_bias, fc_out_weight, fc_out_bias,
):
    parts = call_layer(
        positions,
        tokens[0],
        cotangent[0],
        ln_gain[None],
        ln_bias[None],
        qkv_weight.transpose(1, 0, 2),
        out_weight,
        fc_in_weight,
        fc_in_bias[None],
        fc_out_weight,
        fc_out_bias[None],
    )
    (
        fc_out_grad, fc_in_grad, qkv_grad, out_grad, block_out, tokens_grad,
        gain_grad, bias_grad, fc_in_bias_grad, fc_out_bias_grad,
    ) = call_widen(*parts)
    return (
        block_out[None],
        tokens_grad[None],
        gain_grad[0],
        bias_grad[0],
        qkv_grad.transpose(1, 0, 2),
        out_grad,
        fc_in_grad,
        fc_in_bias_grad[0],
        fc_out_grad,
        fc_out_bias_grad[0],
    )


def solution(mesh):
    placed = (
        P("seq", "ctx", None), P("seq", "ctx"), P("seq", "ctx", None), P(), P(),
        P(None, None, "tp"), P("tp", None), P(None, "tp"), P("tp"), P("tp", None), P(),
    )
    return jax.shard_map(
        local,
        mesh=mesh,
        in_specs=placed,
        out_specs=(
            P("seq", "ctx", None), P("seq", "ctx", None), P(), P(), P(None, None, "tp"),
            P("tp", None), P(None, "tp"), P("tp"), P("tp", None), P(),
        ),
        check_vma=False,
    )
```

```python
import math
from types import SimpleNamespace

import jax
import jax.numpy as jnp
from jax import lax
from jax.experimental import pallas as pl
from jax.experimental.pallas import tpu as pltpu
from jax.sharding import PartitionSpec as P

HD = 64
ROT = 32
T = 256
D = 1024
L = 512
F = 2048
MESH = pl.DeviceIdType.MESH
BF = jnp.bfloat16
F32 = jnp.float32
EPS = 1e-05
ROWS = (1024, 1024, 1024, 512)
WIDE = (512, 512, 384, 256)
ORDER = ("xz", "xz", "xz", "xz")
Y_FIRST = (True, True, False, False)


def dot(a, b):
    return lax.dot_general(a, b, (((1,), (0,)), ((), ())), preferred_element_type=F32)


def dot_nt(a, b):
    return lax.dot_general(a, b, (((1,), (1,)), ((), ())), preferred_element_type=F32)


def xor(a, b):
    return a + b - 2 * a * b


class Place:
    def __init__(self):
        seq, ctx, tp = lax.axis_index("seq"), lax.axis_index("ctx"), lax.axis_index("tp")
        self.seq, self.ctx, self.tp = seq, ctx, tp
        self.z, self.core, self.x, self.yh = seq // 2, seq % 2, ctx // 2, ctx % 2
        c, x, z = self.core, self.x, self.z
        flip = lambda i: i + 1 - 2 * (i % 2)
        self.sib = (z * 2 + 1 - c, ctx, tp)
        self.other_tp = (seq, ctx, 1 - tp)
        self.y = (seq, x * 2 + 1 - self.yh, tp)
        self.x_one = (seq, flip(x) * 2 + self.yh, tp)
        self.x_three = (seq, (3 - x) * 2 + self.yh, tp)
        self.z_one = (flip(z) * 2 + c, ctx, tp)
        self.z_three = ((3 - z) * 2 + c, ctx, tp)
        c = {"xz": c, "z": 1, "x": 0}
        self.order = [Order(self, c[kind]) for kind in ORDER]


class Order:
    def __init__(self, me, c):
        x, z = me.x, me.z
        pick = lambda a, b: tuple((1 - c) * p + c * q for p, q in zip(a, b))
        u, v = (1 - c) * x + c * z, (1 - c) * z + c * x
        one, three = pick(me.x_one, me.z_one), pick(me.x_three, me.z_three)
        self.before, self.after = (one, three), (three, one)
        flip = u + 1 - 2 * (u % 2)
        self.keep, self.give = (u, u), (3 - u, flip)
        self.their_give, self.their_keep = (lax.rem(u + 2, 4),) * 2, (flip, 3 - u)
        self.v = v
        self.others = []
        for k in range(1, 4):
            to = lax.rem(v + k, 4)
            zz, xx = (1 - c) * to + c * z, (1 - c) * x + c * to
            self.others.append((to, (zz * 2 + me.core, xx * 2 + me.yh, me.tp)))


def remote(src, dst, send, recv, device):
    return pltpu.make_async_remote_copy(
        src_ref=src, dst_ref=dst, send_sem=send, recv_sem=recv, device_id=device, device_id_type=MESH
    )


def rotate(u, cosine, even, odd):
    return u * cosine + pltpu.roll(u, 127, 1) * even + pltpu.roll(u, 1, 1) * odd


def keys(j):
    return slice(j * T, j * T + T)


def tri(r):
    return r * (r + 1) // 2 * T


def layer_kernel(
    pos_h, tok_h, cot_h, gain, lnb, wqkv_h, wout_h, fin_h, finb, fout_h, foutb,
    out_b, out_t, out_s, out_0, out_1, out_2, out_3,
    pos, tok, cot, nrm, xhat, inv, wqkv, wout, fin, fout, tabs, send1, land1, ptile, pland, psm, qg, kv,
    kvt, sbuf, pbuf, atts, aq, send2, land2, sib_att, send3, land3, act_o, act_b, gh_o, gh_b, lf_o, lf_b,
    nrm_t, tps, tpl, g0, g1, g2, g3, l0, l1, l2, l3, r0, r1, r2, r3, t0, t1, t2, t3, y0, y1, y2, y3, w0,
    w1, w2, w3, vs, vw, blk, tgr, in_sem, sib_s, sib_r, all_s, all_r, tp_s, tp_r, rs_s, rs_r, fw_s, fw_r,
    st_s, v_s, v_r, o_s,
):
    me = Place()
    core, ctx = me.core, me.ctx
    g, lands, res, outs = (g0, g1, g2, g3), (l0, l1, l2, l3), (r0, r1, r2, r3), (out_0, out_1, out_2, out_3)
    slots, ybuf, whole_q = (t0, t1, t2, t3), (y0, y1, y2, y3), (w0, w1, w2, w3)

    loads = [
        pltpu.make_async_copy(a, b, in_sem.at[i])
        for i, (a, b) in enumerate(
            (
                (pos_h, pos), (tok_h, tok), (cot_h, cot.at[0]), (wqkv_h, wqkv), (wout_h, wout),
                (fin_h, fin), (fout_h, fout),
            )
        )
    ]
    for copy in loads:
        copy.start()

    barrier = pltpu.get_barrier_semaphore()
    peers = [(me.seq, lax.rem(ctx + k, 8), me.tp) for k in range(1, 8)]
    across = [(lax.rem(me.z + k, 4) * 2 + core, ctx, me.tp) for k in range(1, 4)]
    for device in peers + across + [me.sib, me.other_tp]:
        pl.semaphore_signal(barrier, inc=1, device_id=device, device_id_type=MESH)

    loads[1].wait()

    def norm_rows(i, _):
        rows = pl.ds(pl.multiple_of(i * 64, 64), 64)
        x = tok[rows, :].astype(F32)
        x = x - jnp.mean(x, axis=-1, keepdims=True)
        inv_std = lax.rsqrt(jnp.mean(x * x, axis=-1, keepdims=True) + EPS)
        x = x * inv_std
        xhat[rows, :] = x
        inv[rows, :] = jnp.broadcast_to(inv_std, (64, 128))
        nrm[0, rows, :] = (x * gain[...] + lnb[...]).astype(BF)
        return 0

    lax.fori_loop(0, T // 64, norm_rows, 0)

    loads[0].wait()
    first = pos[0, 0]
    lane = lax.broadcasted_iota(jnp.int32, (T, 128), 1)
    row = lax.broadcasted_iota(jnp.int32, (T, 128), 0)
    in_head = lane % HD
    low_lane = lane < HD
    freq = jnp.exp((in_head // 2).astype(F32) * (-2.0 * math.log(10000.0) / ROT))
    theta = (row + first).astype(F32) * freq
    turning = in_head < ROT
    sine = jnp.where(turning, jnp.sin(theta), 0.0)
    tabs[0] = jnp.where(turning, jnp.cos(theta), 1.0)
    tabs[1] = jnp.where(lane % 2 == 0, -sine, 0.0)
    tabs[2] = jnp.where(lane % 2 == 0, 0.0, sine)
    ptile[...] = jnp.full((8, 128), first, jnp.int32)

    loads[2].wait()
    pl.semaphore_wait(barrier, 12)

    sib_pairs = (
        (cot.at[0], cot.at[1]),
        (nrm.at[0], nrm.at[1]),
        (act_o, act_b.at[1]),
        (gh_o, gh_b.at[1]),
        (land2.at[pl.ds(4 * (1 - core), 4)], sib_att),
        (lf_o, lf_b.at[1]),
    )

    def to_sib(i):
        return remote(*sib_pairs[i], sib_s.at[i], sib_r.at[i], me.sib)

    def to_all(src, dst, i):
        for k in range(1, 8):
            to = lax.rem(ctx + k, 8)
            here = src if i == 0 else src.at[to]
            remote(here, dst.at[ctx], all_s.at[i], all_r.at[i], peers[k - 1]).start()
        dst[ctx] = src[...] if i == 0 else src[ctx]

    def all_seven(dst, i):
        return remote(dst.at[pl.ds(0, 7)], dst.at[pl.ds(0, 7)], all_s.at[i], all_r.at[i], me.sib)

    to_sib(0).start()
    to_sib(1).start()

    loads[3].wait()
    loads[4].wait()
    to_all(ptile, pland, 0)
    normed = nrm[0]
    swap = lambda a: pltpu.roll(a, HD, 1)
    for e in range(4):
        cols = slice(128 * e, 128 * e + 128)
        turn = (tabs[0], tabs[1], tabs[2])
        q = rotate(dot(normed, wqkv[0, :, cols]), *turn) * HD ** (-0.5)
        k = rotate(dot(normed, wqkv[1, :, cols]), *turn)
        v = dot(normed, wqkv[2, :, cols])
        ga = dot_nt(cot[0], wout[cols, :])
        send1[2 * e, :, 0:128] = jnp.where(low_lane, q, swap(ga)).astype(BF)
        send1[2 * e, :, 128:256] = jnp.where(low_lane, k, swap(v)).astype(BF)
        send1[2 * e + 1, :, 0:128] = jnp.where(low_lane, swap(q), ga).astype(BF)
        send1[2 * e + 1, :, 128:256] = jnp.where(low_lane, swap(k), v).astype(BF)
        for d in (2 * e, 2 * e + 1):

            @pl.when(ctx != d)
            def _():
                remote(send1.at[d], land1.at[ctx], all_s.at[1], all_r.at[1], (me.seq, d, me.tp)).start()

    land1[ctx] = send1[ctx]

    loads[5].wait()
    loads[6].wait()
    vs[0] = jnp.zeros((8, D), F32)

    def hidden(half, act_ref, gh_ref, i):
        start = pl.multiple_of(half * 1024 + i * 256, 256)
        here = pl.ds(pl.multiple_of(i * 256, 256), 256)
        u = dot(nrm[0], fin[:, pl.ds(start, 256)]) + finb[:, pl.ds(start, 256)]
        z = math.sqrt(2.0 / math.pi) * (u + 0.044715 * u * u * u)
        t = jnp.tanh(z)
        act_ref[:, here] = (0.5 * u * (1.0 + t)).astype(BF)
        slope = 0.5 * (1.0 + t) + (0.5 * math.sqrt(2.0 / math.pi)) * u * (1.0 - t * t) * (
            1.0 + 3 * 0.044715 * u * u
        )
        grad = dot_nt(cot[0], fout[pl.ds(start, 256), :]) * slope
        low = grad.astype(BF)
        gh_ref[:, here] = low
        vs[0, pl.ds(2 + half, 1), here] = jnp.sum(low.astype(F32), axis=0, keepdims=True)

    def other_half(i, _):
        hidden(1 - core, act_o, gh_o, i)
        return 0

    def own_half(i, _):
        hidden(core, act_b.at[0], gh_b.at[0], i)
        return 0

    lax.fori_loop(0, 4, other_half, 0)
    to_sib(2).start()
    to_sib(3).start()
    lax.fori_loop(0, 4, own_half, 0)

    def turn_over(src, dst):
        def body(i, _):
            here = pl.ds(pl.multiple_of(i * 128, 128), 128)
            for token in range(2):
                dst[token, here, :] = src[token, :, here].T
            return 0

        lax.fori_loop(0, D // 128, body, 0)

    def quarter(m, q):
        return pl.ds(pl.multiple_of(q * (ROWS[m] // 4), ROWS[m] // 4), ROWS[m] // 4)

    def swap_copy(m, h, k):
        o = me.order[m]
        q = (o.their_give, o.their_keep, o.give)[k][h]
        device = o.after[h] if k == 2 else o.before[h]
        return remote(g[m].at[h, quarter(m, q)], lands[m].at[k, h], rs_s.at[m, 0], rs_r.at[m, min(k, 1)], device)

    def arrived(m, ref, i):
        remote(ref, ref, rs_s.at[m, 0], rs_r.at[m, i], me.sib).wait_recv()

    def add(m, h, into, rows, start, *terms):
        block = 64

        def body(i, _):
            here = pl.ds(pl.multiple_of(i * block, block), block)
            total = g[m][h, pl.ds(pl.multiple_of(start + i * block, block), block), :].astype(F32)
            for k in terms:
                total = total + lands[m][k, h, here, :].astype(F32)
            if into is None:
                g[m][h, pl.ds(pl.multiple_of(start + i * block, block), block), :] = total.astype(BF)
            else:
                lands[m][into, h, here, :] = total.astype(BF)
            return 0

        lax.fori_loop(0, rows // block, body, 0)

    def first_sum(m):
        arrived(m, lands[m].at[0], 0)
        for h in range(2):
            add(m, h, None, ROWS[m] // 4, me.order[m].give[h] * (ROWS[m] // 4), 0)
            swap_copy(m, h, 2).start()

    def rows_of(m, v, y, wide):
        n = ROWS[m] // 32
        start = (y * 4 + v) * n if Y_FIRST[m] else (v * 2 + y) * n
        return pl.ds(pl.multiple_of(start, 16), n * wide)

    def along_v(m, ref, i, slot):
        o = me.order[m]
        for to, device in o.others:
            if slot:
                src = ref.at[:, rows_of(m, to, me.yh, 1) if Y_FIRST[m] else rows_of(m, to, 0, 2)]
                dst = slots[m].at[o.v]
            else:
                src = ref.at[:, rows_of(m, o.v, me.yh, 1) if Y_FIRST[m] else rows_of(m, o.v, 0, 2)]
                dst = src
            remote(src, dst, rs_s.at[m, i - 1], rs_r.at[m, i], device).start()

    def along_y(m, ref, i, slot):
        o = me.order[m]
        y = 1 - me.yh if slot else me.yh
        src = ref.at[:, rows_of(m, 0, y, 4) if Y_FIRST[m] else rows_of(m, o.v, y, 1)]
        remote(src, ybuf[m] if slot else src, rs_s.at[m, i - 1], rs_r.at[m, i], me.y).start()

    def sum_v(m, into):
        o = me.order[m]
        here = rows_of(m, o.v, me.yh, 1) if Y_FIRST[m] else rows_of(m, o.v, 0, 2)
        slots[m][o.v] = lands[m][2, :, here, :]
        for h in range(2):
            total = slots[m][0, h].astype(F32)
            for k in range(1, 4):
                total = total + slots[m][k, h].astype(F32)
            into[h, here, :] = total.astype(BF)

    def sum_y(m, into):
        here = rows_of(m, 0, me.yh, 4) if Y_FIRST[m] else rows_of(m, me.order[m].v, me.yh, 1)
        for h in range(2):
            total = lands[m][2, h, here, :].astype(F32) + ybuf[m][h].astype(F32)
            into[h, here, :] = total.astype(BF)

    def three(m):
        return slots[m].at[pl.ds(0, 3)]

    def second_sum(m):
        arrived(m, lands[m].at[pl.ds(1, 2)], 1)
        for h in range(2):
            add(m, h, 2, ROWS[m] // 4, me.order[m].keep[h] * (ROWS[m] // 4), 1, 2)
        (along_y if Y_FIRST[m] else along_v)(m, lands[m].at[2], 2, True)

    def third_sum(m):
        arrived(m, ybuf[m] if Y_FIRST[m] else three(m), 2)
        (sum_y if Y_FIRST[m] else sum_v)(m, lands[m].at[2])
        (along_v if Y_FIRST[m] else along_y)(m, lands[m].at[2], 3, True)

    def fourth_sum(m):
        arrived(m, three(m) if Y_FIRST[m] else ybuf[m], 3)
        (sum_v if Y_FIRST[m] else sum_y)(m, whole_q[m])
        (along_v if Y_FIRST[m] else along_y)(m, whole_q[m], 4, False)

    def zeroth_gather(m):
        arrived(m, three(m) if Y_FIRST[m] else ybuf[m], 4)
        (along_y if Y_FIRST[m] else along_v)(m, whole_q[m], 5, False)

    def hand_over(m, h, src, q):
        there = outs[m].at[core, h, quarter(m, q)]
        remote(src, there, fw_s.at[m], fw_r.at[m], me.sib).start()
        pltpu.make_async_copy(src, there, st_s.at[m]).start()

    def spread(m, h, src, k):
        o = me.order[m]
        device = (o.before if k else o.after)[h]
        remote(src, res[m].at[k, h], rs_s.at[m, 5], rs_r.at[m, 6 + min(k, 1)], device).start()

    def first_gather(m):
        arrived(m, ybuf[m] if Y_FIRST[m] else three(m), 5)
        o = me.order[m]
        for k in range(2):
            for h in range(2):
                spread(m, h, whole_q[m].at[h], k)
        for h in range(2):
            hand_over(m, h, whole_q[m].at[h], o.keep[h])

    def second_gather(m):
        arrived(m, lands[m].at[0], 6)
        o = me.order[m]
        for h in range(2):
            spread(m, h, res[m].at[0, h], 2)
            hand_over(m, h, res[m].at[0, h], o.give[h])

    def third_gather(m):
        arrived(m, lands[m].at[pl.ds(0, 2)], 7)
        o = me.order[m]
        for h in range(2):
            hand_over(m, h, res[m].at[1, h], o.their_keep[h])
            hand_over(m, h, res[m].at[2, h], o.their_give[h])

    def outer(m, left_t, right):
        o = me.order[m]
        for k, qs in enumerate((o.their_give, o.their_keep, o.give, o.keep)):
            for h in range(2):
                rows = quarter(m, qs[h])
                cols = slice(WIDE[m] * h, WIDE[m] * h + WIDE[m])
                total = dot(left_t[0, rows, :], right[0, :, cols]) + dot(left_t[1, rows, :], right[1, :, cols])
                g[m][h, rows, :] = total.astype(BF)
                if k < 2:
                    swap_copy(m, h, k).start()

    act_t = pbuf.at[pl.ds(0, 2 * D)].reshape(2, D, T)
    to_sib(2).wait_recv()
    turn_over(act_b, act_t)
    to_sib(0).wait_recv()
    outer(0, act_t, cot)
    to_sib(1).wait_recv()
    turn_over(nrm, nrm_t)
    to_sib(3).wait_recv()
    outer(1, nrm_t, gh_b)
    vs[0, 4:5, :] = jnp.sum(cot[0].astype(F32), axis=0, keepdims=True)

    all_seven(pland, 0).wait_recv()
    to_scalar = pltpu.make_async_copy(pland, psm, o_s.at[2])
    to_scalar.start()
    all_seven(land1, 1).wait_recv()
    to_scalar.wait()
    rank = [psm[c, 0, 0] // T for c in range(8)]
    for r in range(8):
        at = 0
        for c in range(8):
            at = jnp.where(rank[c] == r, c, at)
        block = land1[at]
        qg[keys(r), :] = block[:, 0:128]
        kv[keys(r), :] = block[:, 128:256]
        kvt[:, keys(r)] = block[:, 128:256].T

    causal = lax.broadcasted_iota(jnp.int32, (T, T), 0) <= lax.broadcasted_iota(jnp.int32, (T, T), 1)
    deltas = [None] * 8

    def split(r):
        both_lanes = qg[keys(r), :]
        zero = jnp.zeros_like(both_lanes)
        return jnp.where(low_lane, both_lanes, zero), jnp.where(low_lane, zero, both_lanes)

    def scores(r):
        q, _ = split(r)
        top = jnp.full((8, T), -1e30, F32)
        for j in range(r + 1):
            s = dot_nt(kv[keys(j), :], q)
            if j == r:
                s = jnp.where(causal, s, -1e30)
            sbuf[r % 2, keys(j), :] = s
            top = jnp.maximum(top, jnp.max(s.reshape(T // 8, 8, T), axis=0))
        return top

    def weigh(r, top):
        top = jnp.max(top, axis=0, keepdims=True)
        total, att = jnp.zeros((8, T), F32), jnp.zeros((HD, T), F32)
        for j in range(r + 1):
            e = jnp.exp(sbuf[r % 2, keys(j), :] - top)
            total = total + jnp.sum(e.reshape(T // 8, 8, T), axis=0)
            low = e.astype(BF)
            pbuf[tri(r) + j * T : tri(r) + j * T + T, :] = low
            att = att + dot(kvt[HD:, keys(j)], low)
        scale = 1.0 / jnp.sum(total, axis=0, keepdims=True)
        att = att * scale
        atts[r] = att.astype(BF)
        both_lanes = qg[keys(r), :]
        ga_t = (both_lanes.T.astype(F32)[HD:, :] * scale).astype(BF)
        deltas[r] = jnp.sum(ga_t.astype(F32) * att, axis=0, keepdims=True)
        ga = jnp.concatenate([jnp.zeros((HD, T), BF), ga_t], axis=0).T
        qg[keys(r), :] = jnp.where(low_lane, both_lanes, ga)

    def back(r):
        q, ga = split(r)
        dq = jnp.zeros((HD, T), F32)
        for j in range(r + 1):
            prob = pbuf[tri(r) + j * T : tri(r) + j * T + T, :]
            dp = dot_nt(kv[keys(j), :], ga)
            ds = (prob.astype(F32) * (dp - deltas[r])).astype(BF)
            update = dot(ds, q) + dot(prob, ga)
            if r == 7:
                sbuf[0, keys(j), 0:128] = update
            else:
                sbuf[0, keys(j), 0:128] += update
            dq = dq + dot(kvt[:HD, keys(j)], ds)
        dq = (dq * HD ** (-0.5)).astype(BF)
        aq[r, 0:256, :] = sbuf[0, keys(r), 0:128].astype(BF)
        aq[r, 256:320, :] = dq[:, 0:128]
        aq[r, 320:384, :] = dq[:, 128:256]

    own, oth = pl.multiple_of(core * 1024, 1024), pl.multiple_of((1 - core) * 1024, 1024)

    def tp_copy(i, j):
        return remote(tps.at[i, j], tpl.at[i, j], tp_s.at[i], tp_r.at[i], me.other_tp)

    def tp_all(i):
        return remote(tps.at[i], tpl.at[i], tp_s.at[i], tp_r.at[i], me.other_tp)

    def mixed(i, _):
        cols = pl.ds(pl.multiple_of(i * 256, 256), 256)
        sbuf[1, cols, :] = dot_nt(gh_b[0], fin[cols, pl.ds(own, 1024)]) + dot_nt(gh_o[...], fin[cols, pl.ds(oth, 1024)])
        return 0

    def gather_heads(half, ref):
        for e in range(2):
            low, high = 4 * half + 2 * e, 4 * half + 2 * e + 1
            t0, t1 = land3[low, 0:256, :].astype(F32), land3[high, 0:256, :].astype(F32)
            dq_t = jnp.concatenate(
                [
                    jnp.concatenate([land3[i, 256:320, :], land3[i, 320:384, :]], axis=1)
                    for i in (low, high)
                ],
                axis=0,
            )
            turn = (tabs[0], -tabs[1], -tabs[2])
            dq = rotate(dq_t.T.astype(F32), *turn)
            dk = rotate(jnp.where(low_lane, t0, swap(t1)), *turn)
            dv = jnp.where(low_lane, swap(t0), t1)
            for j, part in enumerate((dq, dk, dv)):
                ref[:, 256 * j + 128 * e : 256 * j + 128 * e + 128] = part.astype(BF)

    def late(i, _):
        cols = pl.ds(pl.multiple_of(i * 256, 256), 256)
        grad = sbuf[1, cols, :]
        for ref, half in ((lf_b.at[0], core), (lf_o, 1 - core)):
            at = pl.multiple_of(half * 256, 256)
            for j in range(3):
                grad = grad + dot_nt(ref[:, 256 * j : 256 * j + 256], wqkv[j, cols, pl.ds(at, 256)])
        tps[1, i] = grad.astype(BF)
        vs[0, 0:1, cols] = jnp.sum(grad * xhat[:, cols], axis=0, keepdims=True)
        vs[0, 1:2, cols] = jnp.sum(grad, axis=0, keepdims=True)
        return 0

    v_to = (me.sib, me.y, me.x_one, me.x_three, me.z_one, me.z_three, me.other_tp)

    def v_copy(i):
        return remote(vs.at[i], vw.at[i], v_s.at[0], v_r.at[i], v_to[i])

    def v_step(i):
        v_copy(i).wait_recv()
        total = vs[i] + vw[i]
        if i == 6:
            here = lax.broadcasted_iota(jnp.int32, (8, D), 0) < 2
            out_s[...] = jnp.where(here, total, vs[i])
        else:
            vs[i + 1] = total
            v_copy(i + 1).start()

    def finish(i, _):
        rows = pl.ds(pl.multiple_of(i * 32, 32), 32)

        def whole(k):
            parts = [tps[k, j, rows, :].astype(F32) + tpl[k, j, rows, :].astype(F32) for j in range(4)]
            return jnp.concatenate(parts, axis=1).astype(BF).astype(F32)

        blk[rows, :] = (tok[rows, :].astype(F32) + whole(0) + foutb[...]).astype(BF)
        grad = whole(1)
        scaled = grad * gain[...]
        x = xhat[rows, :]
        mean_one = jnp.mean(scaled, axis=-1, keepdims=True)
        mean_two = jnp.mean(scaled * x, axis=-1, keepdims=True)
        inv_std = inv[rows, 0:1]
        tgr[rows, :] = cot[0, rows, :].astype(F32) + inv_std * (scaled - mean_one - x * mean_two)
        return 0

    to_out = [pltpu.make_async_copy(blk, out_b, o_s.at[0]), pltpu.make_async_copy(tgr, out_t, o_s.at[1])]

    def branch(i, _):
        cols = pl.ds(pl.multiple_of(i * 256, 256), 256)
        part = dot(act_b[0], fout[pl.ds(own, 1024), cols]) + dot(act_o[...], fout[pl.ds(oth, 1024), cols])
        tps[0, i] = (part + dot(lf_o[:, 0:L], wout[:, cols])).astype(BF)
        return 0

    first_sum(1)
    ahead = scores(7)
    for r in range(7, -1, -1):
        now = ahead
        if r:
            ahead = scores(r - 1)
        weigh(r, now)
    for c in range(8):
        send2[c] = atts[rank[c]]
    to_all(send2, land2, 2)
    back(7)
    back(6)
    first_sum(0)
    second_sum(1)
    back(5)
    back(4)
    lax.fori_loop(0, 4, mixed, 0)
    back(3)
    back(2)
    back(1)
    back(0)
    for c in range(8):
        send3[c] = aq[rank[c]]
    to_all(send3, land3, 3)
    all_seven(land2, 2).wait_recv()
    to_sib(4).start()
    lf_o[:, 0:L] = land2[...].reshape(L, T).T
    lax.fori_loop(0, 4, branch, 0)
    third_sum(1)
    to_sib(4).wait_recv()
    mine = land2[pl.ds(4 * core, 4)].reshape(T, T)
    theirs = sib_att[...].reshape(T, T)
    for h in range(2):
        for q in range(2):
            cols = slice(512 * h + 256 * q, 512 * h + 256 * q + 256)
            g3[h, 256 * q : 256 * q + 256, :] = (dot(mine, cot[0, :, cols]) + dot(theirs, cot[1, :, cols])).astype(BF)
    for k in range(2):
        for h in range(2):
            swap_copy(3, h, k).start()
    second_sum(0)
    fourth_sum(1)
    first_sum(3)
    tp_copy(0, 2).start()
    all_seven(land3, 3).wait_recv()
    gather_heads(1 - core, lf_o)
    to_sib(5).start()
    gather_heads(core, lf_b.at[0])
    to_sib(5).wait_recv()
    outer(2, nrm_t, lf_b)
    zeroth_gather(1)
    third_sum(0)
    lax.fori_loop(0, 4, late, 0)
    v_copy(0).start()
    first_sum(2)
    v_step(0)
    tp_copy(1, 0).start()
    fourth_sum(0)
    tp_copy(0, 0).start()
    second_sum(3)
    v_step(1)
    second_sum(2)
    first_gather(1)
    zeroth_gather(0)
    v_step(2)
    second_gather(1)
    third_sum(2)
    v_step(3)
    first_gather(0)
    third_sum(3)
    fourth_sum(2)
    fourth_sum(3)
    tp_copy(0, 1).start()
    tp_copy(1, 1).start()
    zeroth_gather(2)
    zeroth_gather(3)
    tp_copy(1, 3).start()
    v_step(4)
    third_gather(1)
    second_gather(0)
    first_gather(2)
    tp_copy(0, 3).start()
    tp_copy(1, 2).start()
    v_step(5)
    first_gather(3)
    third_gather(0)
    second_gather(2)
    second_gather(3)
    third_gather(2)
    third_gather(3)
    tp_all(0).wait_recv()
    tp_all(1).wait_recv()
    lax.fori_loop(0, T // 32, finish, 0)
    to_out[0].start()
    to_out[1].start()
    v_step(6)
    for m in range(4):
        one, other = (ybuf[m], three(m)) if Y_FIRST[m] else (three(m), ybuf[m])
        for i, ref in enumerate((lands[m], one, other, other, one, lands[m])):
            remote(ref, ref, rs_s.at[m, i], rs_r.at[m, 0], me.sib).wait_send()
        half_out = outs[m].at[1 - core]
        remote(g[m], half_out, fw_s.at[m], fw_r.at[m], me.sib).wait()
        pltpu.make_async_copy(g[m], outs[m].at[core], st_s.at[m]).wait()
    for i in range(6):
        to_sib(i).wait_send()
    all_seven(pland, 0).wait_send()
    all_seven(land1, 1).wait_send()
    all_seven(land2, 2).wait_send()
    all_seven(land3, 3).wait_send()
    for i in range(2):
        tp_all(i).wait_send()
        to_out[i].wait()
    remote(vs, vw, v_s.at[0], v_r.at[0], me.sib).wait_send()


def call_layer(*args):
    anyspace = pl.BlockSpec(memory_space=pl.ANY)
    vmem = pl.BlockSpec(memory_space=pltpu.VMEM)
    dma = lambda *shape: pltpu.SemaphoreType.DMA(shape)
    V = pltpu.VMEM
    return pl.pallas_call(
        layer_kernel,
        name="layer",
        out_shape=(
            jax.ShapeDtypeStruct((T, D), BF),
            jax.ShapeDtypeStruct((T, D), F32),
            jax.ShapeDtypeStruct((8, D), F32),
        )
        + tuple(jax.ShapeDtypeStruct((2, 2, ROWS[m], WIDE[m]), BF) for m in range(4)),
        in_specs=[anyspace] * 3 + [vmem, vmem, anyspace, anyspace, anyspace, vmem, anyspace, vmem],
        out_specs=(anyspace, anyspace, vmem) + (anyspace,) * 4,
        scratch_shapes=[
            pltpu.SMEM((1, T), jnp.int32), V((T, D), BF), V((2, T, D), BF), V((2, T, D), BF), V((T, D), F32),
            V((T, 128), F32), V((3, D, L), BF), V((L, D), BF), V((D, F), BF), V((F, D), BF), V((3, T, 128), F32),
            V((8, T, 256), BF), V((8, T, 256), BF), V((8, 128), jnp.int32), V((8, 8, 128), jnp.int32),
            pltpu.SMEM((8, 8, 128), jnp.int32), V((8 * T, 128), BF), V((8 * T, 128), BF), V((128, 8 * T), BF),
            V((2, 8 * T, T), F32), V((36 * T, T), BF), V((8, HD, T), BF), V((8, 384, 128), BF), V((8, HD, T), BF),
            V((8, HD, T), BF), V((4, HD, T), BF), V((8, 384, 128), BF), V((8, 384, 128), BF), V((T, 1024), BF),
            V((2, T, 1024), BF), V((T, 1024), BF), V((2, T, 1024), BF), V((T, 768), BF), V((2, T, 768), BF),
            V((2, D, T), BF), V((2, 4, T, T), BF), V((2, 4, T, T), BF), V((2, 1024, 512), BF),
            V((2, 1024, 512), BF), V((2, 1024, 384), BF), V((2, 512, 256), BF), V((3, 2, 256, 512), BF),
            V((3, 2, 256, 512), BF), V((3, 2, 256, 384), BF), V((3, 2, 128, 256), BF), V((3, 2, 256, 512), BF),
            V((3, 2, 256, 512), BF), V((3, 2, 256, 384), BF), V((3, 2, 128, 256), BF), V((4, 2, 32, 512), BF),
            V((4, 2, 32, 512), BF), V((4, 2, 64, 384), BF), V((4, 2, 32, 256), BF), V((2, 128, 512), BF),
            V((2, 128, 512), BF), V((2, 32, 384), BF), V((2, 16, 256), BF), V((2, 256, 512), BF),
            V((2, 256, 512), BF), V((2, 256, 384), BF), V((2, 128, 256), BF), V((7, 8, D), F32), V((7, 8, D), F32),
            V((T, D), BF), V((T, D), F32), dma(7), dma(6), dma(6), dma(4), dma(4), dma(2), dma(2), dma(4, 6),
            dma(4, 8), dma(4), dma(4), dma(4), dma(1), dma(7), dma(3),
        ],
        compiler_params=pltpu.CompilerParams(
            collective_id=0, has_side_effects=True, vmem_limit_bytes=63 * 2**20
        ),
    )(*args)


def widen_kernel(
    a, b, c, d, block, grads, small,
    fc_out, fc_in, qkv, out, block_out, tokens_grad, gain, bias, fc_in_bias, fc_out_bias,
    va, vb, vc, vd, wa, wb, wc, wd, vblk, vtgr, read, write,
):
    def reads(i):
        core, part = i // 4, i % 4
        rows = lambda n, k: pl.ds(pl.multiple_of(k * n, n), n)
        return (
            pltpu.make_async_copy(a.at[core, :, rows(256, part)], va.at[core, :, rows(256, part)], read.at[0, i]),
            pltpu.make_async_copy(b.at[:, :, rows(128, i)], vb.at[:, :, rows(128, i)], read.at[1, i]),
            pltpu.make_async_copy(c.at[:, :, rows(128, i)], vc.at[:, :, rows(128, i)], read.at[2, i]),
            pltpu.make_async_copy(d.at[core, :, :, rows(64, part)], vd.at[core, :, :, rows(64, part)], read.at[3, i]),
        )

    def issue(i, _):
        for copy in reads(i):
            copy.start()
        return 0

    lax.fori_loop(0, 8, issue, 0)
    two = [pltpu.make_async_copy(block, vblk, write.at[6]), pltpu.make_async_copy(grads, vtgr, write.at[7])]
    for copy in two:
        copy.start()
    gain[...] = small[0:1, :]
    bias[...] = small[1:2, :]
    fc_in_bias[:, 0:1024] = small[2:3, :]
    fc_in_bias[:, 1024:2048] = small[3:4, :]
    fc_out_bias[...] = small[4:5, :]

    def step(i, _):
        core, part = i // 4, i % 4
        copies = reads(i)
        copies[0].wait()
        here, there = pl.ds(pl.multiple_of(i * 256, 256), 256), pl.ds(pl.multiple_of(part * 256, 256), 256)
        for half in range(2):
            wa[here, 512 * half : 512 * half + 512] = va[core, half, there, :].astype(F32)
        pltpu.make_async_copy(wa.at[here], fc_out.at[here], write.at[0]).start()
        copies[1].wait()
        here = pl.ds(pl.multiple_of(i * 128, 128), 128)
        for k in range(2):
            for half in range(2):
                start = 1024 * k + 512 * half
                wb[here, start : start + 512] = vb[k, half, here, :].astype(F32)
        pltpu.make_async_copy(wb.at[here], fc_in.at[here], write.at[1]).start()
        copies[2].wait()
        for k in range(2):
            at = 256 * k
            wc[0, here, at : at + 256] = vc[k, 0, here, 0:256].astype(F32)
            wc[1, here, at : at + 128] = vc[k, 0, here, 256:384].astype(F32)
            wc[1, here, at + 128 : at + 256] = vc[k, 1, here, 0:128].astype(F32)
            wc[2, here, at : at + 256] = vc[k, 1, here, 128:384].astype(F32)
        pltpu.make_async_copy(wc.at[:, here], qkv.at[:, here], write.at[2]).start()
        copies[3].wait()
        here, there = pl.ds(pl.multiple_of(i * 64, 64), 64), pl.ds(pl.multiple_of(part * 64, 64), 64)
        for half in range(2):
            for k in range(2):
                start = 512 * half + 256 * k
                wd[here, start : start + 256] = vd[core, half, k, there, :].astype(F32)
        pltpu.make_async_copy(wd.at[here], out.at[here], write.at[3]).start()
        return 0

    lax.fori_loop(0, 8, step, 0)
    whole = [
        pltpu.make_async_copy(src, dst, write.at[i])
        for i, (src, dst) in enumerate(
            ((wa, fc_out), (wb, fc_in), (wc, qkv), (wd, out), (vblk, block_out), (vtgr, tokens_grad))
        )
    ]
    for i in range(2):
        two[i].wait()
        whole[4 + i].start()
    for copy in whole:
        copy.wait()


def call_widen(block, grads, small, a, b, c, d):
    shape, V = jax.ShapeDtypeStruct, pltpu.VMEM
    anyspace, vmem = pl.BlockSpec(memory_space=pl.ANY), pl.BlockSpec(memory_space=pltpu.VMEM)
    return pl.pallas_call(
        widen_kernel,
        name="widen",
        in_specs=[anyspace] * 6 + [vmem],
        out_specs=(anyspace,) * 6 + (vmem,) * 4,
        out_shape=(
            shape((F, D), F32), shape((D, F), F32), shape((3, D, L), F32), shape((L, D), F32),
            shape((T, D), BF), shape((T, D), F32),
            shape((1, D), F32), shape((1, D), F32), shape((1, F), F32), shape((1, D), F32),
        ),
        scratch_shapes=[
            V((2, 2, 1024, 512), BF), V((2, 2, 1024, 512), BF), V((2, 2, 1024, 384), BF), V((2, 2, 2, 256, 256), BF),
            V((F, D), F32), V((D, F), F32), V((3, D, L), F32), V((L, D), F32),
            V((T, D), BF), V((T, D), F32),
            pltpu.SemaphoreType.DMA((4, 8)), pltpu.SemaphoreType.DMA((8,)),
        ],
        compiler_params=pltpu.CompilerParams(vmem_limit_bytes=60 * 2**20),
    )(a, b, c, d.reshape(2, 2, 2, 256, 256), block, grads, small)


def local(
    tokens, positions, cotangent, ln_gain, ln_bias, qkv_weight, out_weight,
    fc_in_weight, fc_in_bias, fc_out_weight, fc_out_bias,
):
    parts = call_layer(
        positions,
        tokens[0],
        cotangent[0],
        ln_gain[None],
        ln_bias[None],
        qkv_weight.transpose(1, 0, 2),
        out_weight,
        fc_in_weight,
        fc_in_bias[None],
        fc_out_weight,
        fc_out_bias[None],
    )
    (
        fc_out_grad, fc_in_grad, qkv_grad, out_grad, block_out, tokens_grad,
        gain_grad, bias_grad, fc_in_bias_grad, fc_out_bias_grad,
    ) = call_widen(*parts)
    return (
        block_out[None],
        tokens_grad[None],
        gain_grad[0],
        bias_grad[0],
        qkv_grad.transpose(1, 0, 2),
        out_grad,
        fc_in_grad,
        fc_in_bias_grad[0],
        fc_out_grad,
        fc_out_bias_grad[0],
    )


def solution(mesh):
    placed = (
        P("seq", "ctx", None), P("seq", "ctx"), P("seq", "ctx", None), P(), P(),
        P(None, None, "tp"), P("tp", None), P(None, "tp"), P("tp"), P("tp", None), P(),
    )
    return jax.shard_map(
        local,
        mesh=mesh,
        in_specs=placed,
        out_specs=(
            P("seq", "ctx", None), P("seq", "ctx", None), P(), P(), P(None, None, "tp"),
            P("tp", None), P(None, "tp"), P("tp"), P("tp", None), P(),
        ),
        check_vma=False,
    )
```

```python
import math
from types import SimpleNamespace

import jax
import jax.numpy as jnp
from jax import lax
from jax.experimental import pallas as pl
from jax.experimental.pallas import tpu as pltpu
from jax.sharding import PartitionSpec as P

HD = 64
ROT = 32
T = 256
D = 1024
L = 512
F = 2048
MESH = pl.DeviceIdType.MESH
BF = jnp.bfloat16
F32 = jnp.float32
EPS = 1e-05
ROWS = (1024, 1024, 1024, 1024)
WIDE = (512, 512, 256, 256)
ORDER = ("xz", "xz", "xz", "xz")
Y_FIRST = (1, 1, 8, 8)


def dot(a, b):
    return lax.dot_general(a, b, (((1,), (0,)), ((), ())), preferred_element_type=F32)


def dot_nt(a, b):
    return lax.dot_general(a, b, (((1,), (1,)), ((), ())), preferred_element_type=F32)


def xor(a, b):
    return a + b - 2 * a * b


class Place:
    def __init__(self):
        seq, ctx, tp = lax.axis_index("seq"), lax.axis_index("ctx"), lax.axis_index("tp")
        self.seq, self.ctx, self.tp = seq, ctx, tp
        self.z, self.core, self.x, self.yh = seq // 2, seq % 2, ctx // 2, ctx % 2
        c, x, z = self.core, self.x, self.z
        flip = lambda i: i + 1 - 2 * (i % 2)
        self.sib = (z * 2 + 1 - c, ctx, tp)
        self.other_tp = (seq, ctx, 1 - tp)
        self.y = (seq, x * 2 + 1 - self.yh, tp)
        self.x_one = (seq, flip(x) * 2 + self.yh, tp)
        self.x_three = (seq, (3 - x) * 2 + self.yh, tp)
        self.z_one = (flip(z) * 2 + c, ctx, tp)
        self.z_three = ((3 - z) * 2 + c, ctx, tp)
        c = {"xz": c, "z": 1, "x": 0}
        self.order = [Order(self, c[kind]) for kind in ORDER]


class Order:
    def __init__(self, me, c):
        x, z = me.x, me.z
        pick = lambda a, b: tuple((1 - c) * p + c * q for p, q in zip(a, b))
        u, v = (1 - c) * x + c * z, (1 - c) * z + c * x
        one, three = pick(me.x_one, me.z_one), pick(me.x_three, me.z_three)
        self.before, self.after = (one, three), (three, one)
        flip = u + 1 - 2 * (u % 2)
        self.keep, self.give = (u, u), (3 - u, flip)
        self.their_give, self.their_keep = (lax.rem(u + 2, 4),) * 2, (flip, 3 - u)
        self.v = v
        self.others, self.seven = [], []
        for k in range(1, 4):
            to = lax.rem(v + k, 4)
            zz, xx = (1 - c) * to + c * z, (1 - c) * x + c * to
            self.others.append((to, (zz * 2 + me.core, xx * 2 + me.yh, me.tp)))
        self.place = v * 2 + me.yh
        for k in range(1, 8):
            to = lax.rem(self.place + k, 8)
            there = to // 2
            zz, xx = (1 - c) * there + c * z, (1 - c) * x + c * there
            self.seven.append((to, (zz * 2 + me.core, xx * 2 + to % 2, me.tp)))


def remote(src, dst, send, recv, device):
    return pltpu.make_async_remote_copy(
        src_ref=src, dst_ref=dst, send_sem=send, recv_sem=recv, device_id=device, device_id_type=MESH
    )


def rotate(u, cosine, even, odd):
    return u * cosine + pltpu.roll(u, 127, 1) * even + pltpu.roll(u, 1, 1) * odd


def keys(j):
    return slice(j * T, j * T + T)


def tri(r):
    return r * (r + 1) // 2 * T


def layer_kernel(
    pos_h, tok_h, cot_h, gain, lnb, wqkv_h, wout_h, fin_h, finb, fout_h, foutb,
    out_b, out_t, out_s, out_0, out_1, out_2, out_3,
    pos, tok, cot, nrm, xhat, inv, wqkv, wout, fin, fout, tabs, send1, land1, ptile, pland, psm, qg, kv,
    kvt, sbuf, pbuf, dvt, atts, aq, send2, land2, sib_att, send3, land3, act_o, act_b, gh_o, gh_b, lf_o,
    lf_b, nrm_t, tps, tpl, g0, g1, g2, g3, l0, l1, l2, l3, r0, r1, r2, r3, t0, t1, t2, t3, y0, y1, y2, y3,
    w0, w1, w2, w3, vs, vw, blk, tgr, in_sem, sib_s, sib_r, all_s, all_r, tp_s, tp_r, rs_s, rs_r, fw_s,
    fw_r, st_s, v_s, v_r, o_s,
):
    me = Place()
    core, ctx = me.core, me.ctx
    g, lands, res, outs = (g0, g1, g2, g3), (l0, l1, l2, l3), (r0, r1, r2, r3), (out_0, out_1, out_2, out_3)
    slots, ybuf, whole_q = (t0, t1, t2, t3), (y0, y1, y2, y3), (w0, w1, w2, w3)

    loads = [
        pltpu.make_async_copy(a, b, in_sem.at[i])
        for i, (a, b) in enumerate(
            (
                (pos_h, pos), (tok_h, tok), (cot_h, cot.at[0]), (wqkv_h, wqkv), (wout_h, wout),
                (fin_h, fin), (fout_h, fout),
            )
        )
    ]
    for copy in loads:
        copy.start()

    barrier = pltpu.get_barrier_semaphore()
    peers = [(me.seq, lax.rem(ctx + k, 8), me.tp) for k in range(1, 8)]
    across = [(lax.rem(me.z + k, 4) * 2 + core, me.x * 2 + yh, me.tp) for k in range(1, 4) for yh in range(2)]
    for device in peers + across + [me.sib, me.other_tp]:
        pl.semaphore_signal(barrier, inc=1, device_id=device, device_id_type=MESH)

    loads[1].wait()

    def norm_rows(i, _):
        rows = pl.ds(pl.multiple_of(i * 64, 64), 64)
        x = tok[rows, :].astype(F32)
        x = x - jnp.mean(x, axis=-1, keepdims=True)
        inv_std = lax.rsqrt(jnp.mean(x * x, axis=-1, keepdims=True) + EPS)
        x = x * inv_std
        xhat[rows, :] = x
        inv[rows, :] = jnp.broadcast_to(inv_std, (64, 128))
        nrm[0, rows, :] = (x * gain[...] + lnb[...]).astype(BF)
        return 0

    lax.fori_loop(0, T // 64, norm_rows, 0)

    loads[0].wait()
    first = pos[0, 0]
    lane = lax.broadcasted_iota(jnp.int32, (T, 128), 1)
    row = lax.broadcasted_iota(jnp.int32, (T, 128), 0)
    in_head = lane % HD
    low_lane = lane < HD
    freq = jnp.exp((in_head // 2).astype(F32) * (-2.0 * math.log(10000.0) / ROT))
    theta = (row + first).astype(F32) * freq
    turning = in_head < ROT
    sine = jnp.where(turning, jnp.sin(theta), 0.0)
    tabs[0] = jnp.where(turning, jnp.cos(theta), 1.0)
    tabs[1] = jnp.where(lane % 2 == 0, -sine, 0.0)
    tabs[2] = jnp.where(lane % 2 == 0, 0.0, sine)
    ptile[...] = jnp.full((8, 128), first, jnp.int32)

    loads[2].wait()
    pl.semaphore_wait(barrier, 15)

    sib_pairs = (
        (cot.at[0], cot.at[1]),
        (nrm.at[0], nrm.at[1]),
        (act_o, act_b.at[1]),
        (gh_o, gh_b.at[1]),
        (land2.at[pl.ds(4 * (1 - core), 4)], sib_att),
        (lf_o, lf_b.at[1]),
    )

    def to_sib(i):
        return remote(*sib_pairs[i], sib_s.at[i], sib_r.at[i], me.sib)

    def to_all(src, dst, i):
        for k in range(1, 8):
            to = lax.rem(ctx + k, 8)
            here = src if i == 0 else src.at[to]
            remote(here, dst.at[ctx], all_s.at[i], all_r.at[i], peers[k - 1]).start()
        dst[ctx] = src[...] if i == 0 else src[ctx]

    def all_seven(dst, i):
        return remote(dst.at[pl.ds(0, 7)], dst.at[pl.ds(0, 7)], all_s.at[i], all_r.at[i], me.sib)

    to_sib(0).start()
    to_sib(1).start()

    loads[3].wait()
    loads[4].wait()
    to_all(ptile, pland, 0)
    normed = nrm[0]
    swap = lambda a: pltpu.roll(a, HD, 1)
    for e in range(4):
        cols = slice(128 * e, 128 * e + 128)
        turn = (tabs[0], tabs[1], tabs[2])
        q = rotate(dot(normed, wqkv[0, :, cols]), *turn) * HD ** (-0.5)
        k = rotate(dot(normed, wqkv[1, :, cols]), *turn)
        v = dot(normed, wqkv[2, :, cols])
        ga = dot_nt(cot[0], wout[cols, :])
        send1[2 * e, :, 0:128] = jnp.where(low_lane, q, swap(ga)).astype(BF)
        send1[2 * e, :, 128:256] = jnp.where(low_lane, k, swap(v)).astype(BF)
        send1[2 * e + 1, :, 0:128] = jnp.where(low_lane, swap(q), ga).astype(BF)
        send1[2 * e + 1, :, 128:256] = jnp.where(low_lane, swap(k), v).astype(BF)
        for d in (2 * e, 2 * e + 1):

            @pl.when(ctx != d)
            def _():
                remote(send1.at[d], land1.at[ctx], all_s.at[1], all_r.at[1], (me.seq, d, me.tp)).start()

    land1[ctx] = send1[ctx]

    loads[5].wait()
    loads[6].wait()
    vs[0] = jnp.zeros((8, D), F32)

    def hidden(half, act_ref, gh_ref, i):
        start = pl.multiple_of(half * 1024 + i * 256, 256)
        here = pl.ds(pl.multiple_of(i * 256, 256), 256)
        u = dot(nrm[0], fin[:, pl.ds(start, 256)]) + finb[:, pl.ds(start, 256)]
        z = math.sqrt(2.0 / math.pi) * (u + 0.044715 * u * u * u)
        t = jnp.tanh(z)
        act_ref[:, here] = (0.5 * u * (1.0 + t)).astype(BF)
        slope = 0.5 * (1.0 + t) + (0.5 * math.sqrt(2.0 / math.pi)) * u * (1.0 - t * t) * (
            1.0 + 3 * 0.044715 * u * u
        )
        grad = dot_nt(cot[0], fout[pl.ds(start, 256), :]) * slope
        low = grad.astype(BF)
        gh_ref[:, here] = low
        vs[0, pl.ds(2 + half, 1), here] = jnp.sum(low.astype(F32), axis=0, keepdims=True)

    def other_half(i, _):
        hidden(1 - core, act_o, gh_o, i)
        return 0

    def own_half(i, _):
        hidden(core, act_b.at[0], gh_b.at[0], i)
        return 0

    lax.fori_loop(0, 4, other_half, 0)
    to_sib(2).start()
    to_sib(3).start()
    lax.fori_loop(0, 4, own_half, 0)

    def turn_over(src, dst):
        def body(i, _):
            here = pl.ds(pl.multiple_of(i * 128, 128), 128)
            for token in range(2):
                dst[token, here, :] = src[token, :, here].T
            return 0

        lax.fori_loop(0, D // 128, body, 0)

    def quarter(m, q):
        return pl.ds(pl.multiple_of(q * (ROWS[m] // 4), ROWS[m] // 4), ROWS[m] // 4)

    def swap_copy(m, h, k):
        o = me.order[m]
        q = (o.their_give, o.their_keep, o.give)[k][h]
        device = o.after[h] if k == 2 else o.before[h]
        return remote(g[m].at[h, quarter(m, q)], lands[m].at[k, h], rs_s.at[m, 0], rs_r.at[m, min(k, 1)], device)

    def arrived(m, ref, i):
        remote(ref, ref, rs_s.at[m, 0], rs_r.at[m, i], me.sib).wait_recv()

    def add(m, h, into, rows, start, *terms):
        block = 64

        def body(i, _):
            here = pl.ds(pl.multiple_of(i * block, block), block)
            total = g[m][h, pl.ds(pl.multiple_of(start + i * block, block), block), :].astype(F32)
            for k in terms:
                total = total + lands[m][k, h, here, :].astype(F32)
            if into is None:
                g[m][h, pl.ds(pl.multiple_of(start + i * block, block), block), :] = total.astype(BF)
            else:
                lands[m][into, h, here, :] = total.astype(BF)
            return 0

        lax.fori_loop(0, rows // block, body, 0)

    def first_sum(m):
        arrived(m, lands[m].at[0], 0)
        for h in range(2):
            add(m, h, None, ROWS[m] // 4, me.order[m].give[h] * (ROWS[m] // 4), 0)
            swap_copy(m, h, 2).start()

    def rows_of(m, v, y, wide):
        n = ROWS[m] // 32
        start = (y * 4 + v) * n if Y_FIRST[m] == 1 else (v * 2 + y) * n
        return pl.ds(pl.multiple_of(start, 16), n * wide)

    def along_v(m, ref, i, slot):
        o = me.order[m]
        for to, device in o.others:
            if slot:
                src = ref.at[:, rows_of(m, to, me.yh, 1) if Y_FIRST[m] == 1 else rows_of(m, to, 0, 2)]
                dst = slots[m].at[o.v]
            else:
                src = ref.at[:, rows_of(m, o.v, me.yh, 1) if Y_FIRST[m] == 1 else rows_of(m, o.v, 0, 2)]
                dst = src
            remote(src, dst, rs_s.at[m, i - 1], rs_r.at[m, i], device).start()

    def along_y(m, ref, i, slot):
        o = me.order[m]
        y = 1 - me.yh if slot else me.yh
        src = ref.at[:, rows_of(m, 0, y, 4) if Y_FIRST[m] == 1 else rows_of(m, o.v, y, 1)]
        remote(src, ybuf[m] if slot else src, rs_s.at[m, i - 1], rs_r.at[m, i], me.y).start()

    def sum_v(m, into):
        o = me.order[m]
        here = rows_of(m, o.v, me.yh, 1) if Y_FIRST[m] == 1 else rows_of(m, o.v, 0, 2)
        slots[m][o.v] = lands[m][2, :, here, :]
        for h in range(2):
            total = slots[m][0, h].astype(F32)
            for k in range(1, 4):
                total = total + slots[m][k, h].astype(F32)
            into[h, here, :] = total.astype(BF)

    def sum_y(m, into):
        here = rows_of(m, 0, me.yh, 4) if Y_FIRST[m] == 1 else rows_of(m, me.order[m].v, me.yh, 1)
        for h in range(2):
            total = lands[m][2, h, here, :].astype(F32) + ybuf[m][h].astype(F32)
            into[h, here, :] = total.astype(BF)

    def eighth(m, place):
        n = ROWS[m] // 32
        return pl.ds(pl.multiple_of(place * n, n), n)

    def sum_seven(m):
        arrived(m, slots[m].at[pl.ds(0, 7)], 2)
        o = me.order[m]
        here = eighth(m, o.place)
        slots[m][o.place] = lands[m][2, :, here, :]
        for h in range(2):
            total = slots[m][0, h].astype(F32)
            for k in range(1, 8):
                total = total + slots[m][k, h].astype(F32)
            whole_q[m][h, here, :] = total.astype(BF)
        piece = whole_q[m].at[:, here]
        for to, device in o.seven:
            remote(piece, piece, rs_s.at[m, 2], rs_r.at[m, 5], device).start()

    def three(m):
        return slots[m].at[pl.ds(0, 3)]

    def second_sum(m):
        arrived(m, lands[m].at[pl.ds(1, 2)], 1)
        for h in range(2):
            add(m, h, 2, ROWS[m] // 4, me.order[m].keep[h] * (ROWS[m] // 4), 1, 2)
        if Y_FIRST[m] == 8:
            o = me.order[m]
            for to, device in o.seven:
                piece = lands[m].at[2, :, eighth(m, to)]
                remote(piece, slots[m].at[o.place], rs_s.at[m, 1], rs_r.at[m, 2], device).start()
            return
        (along_y if Y_FIRST[m] == 1 else along_v)(m, lands[m].at[2], 2, True)

    def third_sum(m):
        if Y_FIRST[m] == 8:
            return sum_seven(m)
        arrived(m, ybuf[m] if Y_FIRST[m] == 1 else three(m), 2)
        (sum_y if Y_FIRST[m] == 1 else sum_v)(m, lands[m].at[2])
        (along_v if Y_FIRST[m] == 1 else along_y)(m, lands[m].at[2], 3, True)

    def fourth_sum(m):
        arrived(m, three(m) if Y_FIRST[m] == 1 else ybuf[m], 3)
        (sum_v if Y_FIRST[m] == 1 else sum_y)(m, whole_q[m])
        (along_v if Y_FIRST[m] == 1 else along_y)(m, whole_q[m], 4, False)

    def zeroth_gather(m):
        arrived(m, three(m) if Y_FIRST[m] == 1 else ybuf[m], 4)
        (along_y if Y_FIRST[m] == 1 else along_v)(m, whole_q[m], 5, False)

    def hand_over(m, h, src, q):
        there = outs[m].at[core, h, quarter(m, q)]
        remote(src, there, fw_s.at[m], fw_r.at[m], me.sib).start()
        pltpu.make_async_copy(src, there, st_s.at[m]).start()

    def spread(m, h, src, k):
        o = me.order[m]
        device = (o.before if k else o.after)[h]
        remote(src, res[m].at[k, h], rs_s.at[m, 5], rs_r.at[m, 6 + min(k, 1)], device).start()

    def first_gather(m):
        last = slots[m].at[pl.ds(0, 7)] if Y_FIRST[m] == 8 else ybuf[m] if Y_FIRST[m] == 1 else three(m)
        arrived(m, last, 5)
        o = me.order[m]
        for k in range(2):
            for h in range(2):
                spread(m, h, whole_q[m].at[h], k)
        for h in range(2):
            hand_over(m, h, whole_q[m].at[h], o.keep[h])

    def second_gather(m):
        arrived(m, lands[m].at[0], 6)
        o = me.order[m]
        for h in range(2):
            spread(m, h, res[m].at[0, h], 2)
            hand_over(m, h, res[m].at[0, h], o.give[h])

    def third_gather(m):
        arrived(m, lands[m].at[pl.ds(0, 2)], 7)
        o = me.order[m]
        for h in range(2):
            hand_over(m, h, res[m].at[1, h], o.their_keep[h])
            hand_over(m, h, res[m].at[2, h], o.their_give[h])

    def outer(m, left_t, right):
        o = me.order[m]
        for k, qs in enumerate((o.their_give, o.their_keep, o.give, o.keep)):
            for h in range(2):
                rows = quarter(m, qs[h])
                cols = slice(WIDE[m] * h, WIDE[m] * h + WIDE[m])
                total = dot(left_t[0, rows, :], right[0, :, cols]) + dot(left_t[1, rows, :], right[1, :, cols])
                g[m][h, rows, :] = total.astype(BF)
                if k < 2:
                    swap_copy(m, h, k).start()

    act_t = pbuf.at[pl.ds(0, 2 * D)].reshape(2, D, T)
    to_sib(2).wait_recv()
    turn_over(act_b, act_t)
    to_sib(0).wait_recv()
    outer(0, act_t, cot)
    to_sib(1).wait_recv()
    turn_over(nrm, nrm_t)
    to_sib(3).wait_recv()
    outer(1, nrm_t, gh_b)
    vs[0, 4:5, :] = jnp.sum(cot[0].astype(F32), axis=0, keepdims=True)

    all_seven(pland, 0).wait_recv()
    to_scalar = pltpu.make_async_copy(pland, psm, o_s.at[2])
    to_scalar.start()
    all_seven(land1, 1).wait_recv()
    to_scalar.wait()
    rank = [psm[c, 0, 0] // T for c in range(8)]
    for r in range(8):
        at = 0
        for c in range(8):
            at = jnp.where(rank[c] == r, c, at)
        block = land1[at]
        qg[keys(r), :] = block[:, 0:128]
        kv[keys(r), :] = block[:, 128:256]
        kvt[:, keys(r)] = block[:, 128:256].T

    causal = lax.broadcasted_iota(jnp.int32, (T, T), 0) <= lax.broadcasted_iota(jnp.int32, (T, T), 1)
    deltas = [None] * 8

    def split(r):
        both_lanes = qg[keys(r), :]
        zero = jnp.zeros_like(both_lanes)
        return jnp.where(low_lane, both_lanes, zero), jnp.where(low_lane, zero, both_lanes)

    def scores(r):
        q, _ = split(r)
        top = jnp.full((8, T), -1e30, F32)
        for j in range(r + 1):
            s = dot_nt(kv[keys(j), :], q)
            if j == r:
                s = jnp.where(causal, s, -1e30)
            sbuf[r % 2, keys(j), :] = s
            top = jnp.maximum(top, jnp.max(s.reshape(T // 8, 8, T), axis=0))
        return top

    def weigh(r, top):
        top = jnp.max(top, axis=0, keepdims=True)
        total, att = jnp.zeros((8, T), F32), jnp.zeros((HD, T), F32)
        for j in range(r + 1):
            e = jnp.exp(sbuf[r % 2, keys(j), :] - top)
            total = total + jnp.sum(e.reshape(T // 8, 8, T), axis=0)
            low = e.astype(BF)
            pbuf[tri(r) + j * T : tri(r) + j * T + T, :] = low
            att = att + dot(kvt[HD:, keys(j)], low)
        scale = 1.0 / jnp.sum(total, axis=0, keepdims=True)
        att = att * scale
        atts[r, 0:HD, :] = att.astype(BF)
        both_lanes = qg[keys(r), :]
        ga_t = (both_lanes.T.astype(F32)[HD:, :] * scale).astype(BF)
        deltas[r] = jnp.sum(ga_t.astype(F32) * att, axis=0, keepdims=True)
        ga = jnp.concatenate([jnp.zeros((HD, T), BF), ga_t], axis=0).T
        qg[keys(r), :] = jnp.where(low_lane, both_lanes, ga)
        for j in range(r + 1):
            update = dot_nt(ga_t, pbuf[tri(r) + j * T : tri(r) + j * T + T, :])
            if r == 7:
                dvt[j] = update
            else:
                dvt[j] += update
        atts[r, HD:, :] = dvt[r].astype(BF)

    def back(r):
        _, ga = split(r)
        q_t = qg[keys(r), :].T[0:HD, :]
        dq = jnp.zeros((HD, T), F32)
        for j in range(r + 1):
            prob = pbuf[tri(r) + j * T : tri(r) + j * T + T, :]
            dp = dot_nt(kv[keys(j), :], ga)
            ds = (prob.astype(F32) * (dp - deltas[r])).astype(BF)
            update = dot_nt(q_t, ds)
            if r == 7:
                sbuf[0, j * HD : j * HD + HD, :] = update
            else:
                sbuf[0, j * HD : j * HD + HD, :] += update
            dq = dq + dot(kvt[:HD, keys(j)], ds)
        aq[r, 0:HD, :] = (dq * HD ** (-0.5)).astype(BF)
        aq[r, HD:, :] = sbuf[0, r * HD : r * HD + HD, :].astype(BF)

    own, oth = pl.multiple_of(core * 1024, 1024), pl.multiple_of((1 - core) * 1024, 1024)

    def tp_copy(i, j):
        return remote(tps.at[i, j], tpl.at[i, j], tp_s.at[i], tp_r.at[i], me.other_tp)

    def tp_all(i):
        return remote(tps.at[i], tpl.at[i], tp_s.at[i], tp_r.at[i], me.other_tp)

    def mixed(i, _):
        cols = pl.ds(pl.multiple_of(i * 256, 256), 256)
        grad = dot_nt(gh_b[0], fin[cols, pl.ds(own, 1024)]) + dot_nt(gh_o[...], fin[cols, pl.ds(oth, 1024)])
        sbuf[1, cols, :] = grad + dot_nt(lf_b[0], wqkv[2, cols, :])
        return 0

    def gather_heads(half, ref):
        turn = (tabs[0], -tabs[1], -tabs[2])
        for e in range(2):
            low, high = 4 * half + 2 * e, 4 * half + 2 * e + 1
            for j in range(2):
                rows = slice(HD * j, HD * j + HD)
                pair = jnp.concatenate([land3[low, rows, :], land3[high, rows, :]], axis=0)
                part = rotate(pair.T.astype(F32), *turn)
                ref[:, 256 * j + 128 * e : 256 * j + 128 * e + 128] = part.astype(BF)

    def late(i, _):
        cols = pl.ds(pl.multiple_of(i * 256, 256), 256)
        grad = sbuf[1, cols, :]
        for ref, half in ((lf_b.at[0], core), (lf_o, 1 - core)):
            at = pl.multiple_of(half * 256, 256)
            for j in range(2):
                grad = grad + dot_nt(ref[:, 256 * j : 256 * j + 256], wqkv[j, cols, pl.ds(at, 256)])
        tps[1, i] = grad.astype(BF)
        vs[0, 0:1, cols] = jnp.sum(grad * xhat[:, cols], axis=0, keepdims=True)
        vs[0, 1:2, cols] = jnp.sum(grad, axis=0, keepdims=True)
        return 0

    v_to = (me.sib, me.y, me.x_one, me.x_three, me.z_one, me.z_three, me.other_tp)

    def v_copy(i):
        return remote(vs.at[i], vw.at[i], v_s.at[0], v_r.at[i], v_to[i])

    def v_step(i):
        v_copy(i).wait_recv()
        total = vs[i] + vw[i]
        if i == 6:
            here = lax.broadcasted_iota(jnp.int32, (8, D), 0) < 2
            out_s[...] = jnp.where(here, total, vs[i])
        else:
            vs[i + 1] = total
            v_copy(i + 1).start()

    def finish(i, _):
        rows = pl.ds(pl.multiple_of(i * 32, 32), 32)

        def whole(k):
            parts = [tps[k, j, rows, :].astype(F32) + tpl[k, j, rows, :].astype(F32) for j in range(4)]
            return jnp.concatenate(parts, axis=1).astype(BF).astype(F32)

        blk[rows, :] = (tok[rows, :].astype(F32) + whole(0) + foutb[...]).astype(BF)
        grad = whole(1)
        scaled = grad * gain[...]
        x = xhat[rows, :]
        mean_one = jnp.mean(scaled, axis=-1, keepdims=True)
        mean_two = jnp.mean(scaled * x, axis=-1, keepdims=True)
        inv_std = inv[rows, 0:1]
        tgr[rows, :] = cot[0, rows, :].astype(F32) + inv_std * (scaled - mean_one - x * mean_two)
        return 0

    to_out = [pltpu.make_async_copy(blk, out_b, o_s.at[0]), pltpu.make_async_copy(tgr, out_t, o_s.at[1])]

    def branch(i, _):
        cols = pl.ds(pl.multiple_of(i * 256, 256), 256)
        part = dot(act_b[0], fout[pl.ds(own, 1024), cols]) + dot(act_o[...], fout[pl.ds(oth, 1024), cols])
        tps[0, i] = (part + dot(lf_o[...], wout[:, cols])).astype(BF)
        return 0

    first_sum(0)
    ahead = scores(7)
    for r in range(7, -1, -1):
        now = ahead
        if r:
            ahead = scores(r - 1)
        weigh(r, now)
    for c in range(8):
        send2[c] = atts[rank[c]]
    to_all(send2, land2, 2)
    back(7)
    back(6)
    back(5)
    back(4)
    first_sum(1)
    back(3)
    back(2)
    second_sum(0)
    back(1)
    back(0)
    for c in range(8):
        send3[c] = aq[rank[c]]
    to_all(send3, land3, 3)
    all_seven(land2, 2).wait_recv()
    to_sib(4).start()
    lf_o[...] = land2[:, 0:HD, :].reshape(L, T).T
    lf_b[0] = land2[:, HD:, :].reshape(L, T).T
    lax.fori_loop(0, 4, branch, 0)
    second_sum(1)
    to_sib(4).wait_recv()
    four = pl.ds(4 * core, 4)
    o3 = me.order[3]
    for k in range(4):
        for h in range(2):
            q = (o3.their_give, o3.their_keep, o3.give, o3.keep)[k][h]
            rows = quarter(3, q)
            if h == 0:
                total = dot_nt(nrm_t[0, rows, :], land2[four, HD:, :].reshape(T, T))
                total = total + dot_nt(nrm_t[1, rows, :], sib_att[:, HD:, :].reshape(T, T))
            else:
                total = dot(land2[four, 0:HD, :].reshape(T, T), cot[0, :, rows])
                total = total + dot(sib_att[:, 0:HD, :].reshape(T, T), cot[1, :, rows])
            g3[h, rows, :] = total.astype(BF)
            if k < 2:
                swap_copy(3, h, k).start()
    tp_copy(0, 0).start()
    third_sum(0)
    lax.fori_loop(0, 4, mixed, 0)
    all_seven(land3, 3).wait_recv()
    gather_heads(1 - core, lf_o)
    to_sib(5).start()
    gather_heads(core, lf_b.at[0])
    lax.fori_loop(0, 4, late, 0)
    v_copy(0).start()
    first_sum(3)
    fourth_sum(0)
    tp_copy(1, 3).start()
    third_sum(1)
    to_sib(5).wait_recv()
    outer(2, nrm_t, lf_b)
    v_step(0)
    second_sum(3)
    zeroth_gather(0)
    v_step(1)
    first_sum(2)
    fourth_sum(1)
    third_sum(3)
    v_step(2)
    first_gather(0)
    second_sum(2)
    zeroth_gather(1)
    first_gather(3)
    v_step(3)
    second_gather(0)
    third_sum(2)
    tp_copy(1, 2).start()
    tp_copy(0, 2).start()
    tp_copy(0, 1).start()
    second_gather(3)
    v_step(4)
    first_gather(1)
    first_gather(2)
    v_step(5)
    tp_copy(1, 0).start()
    tp_copy(1, 1).start()
    third_gather(3)
    second_gather(1)
    third_gather(0)
    tp_copy(0, 3).start()
    second_gather(2)
    v_step(6)
    third_gather(1)
    third_gather(2)
    tp_all(0).wait_recv()
    tp_all(1).wait_recv()
    lax.fori_loop(0, T // 32, finish, 0)
    to_out[0].start()
    to_out[1].start()
    for m in range(4):
        one, other = (ybuf[m], three(m)) if Y_FIRST[m] == 1 else (three(m), ybuf[m])
        every = (lands[m], one, other, other, one, lands[m])
        if Y_FIRST[m] == 8:
            seven = slots[m].at[pl.ds(0, 7)]
            every = (lands[m], seven, seven, None, None, lands[m])
        for i, ref in enumerate(every):
            if ref is None:
                continue
            remote(ref, ref, rs_s.at[m, i], rs_r.at[m, 0], me.sib).wait_send()
        half_out = outs[m].at[1 - core]
        remote(g[m], half_out, fw_s.at[m], fw_r.at[m], me.sib).wait()
        pltpu.make_async_copy(g[m], outs[m].at[core], st_s.at[m]).wait()
    for i in range(6):
        to_sib(i).wait_send()
    all_seven(pland, 0).wait_send()
    all_seven(land1, 1).wait_send()
    all_seven(land2, 2).wait_send()
    all_seven(land3, 3).wait_send()
    for i in range(2):
        tp_all(i).wait_send()
        to_out[i].wait()
    remote(vs, vw, v_s.at[0], v_r.at[0], me.sib).wait_send()


def call_layer(*args):
    anyspace = pl.BlockSpec(memory_space=pl.ANY)
    vmem = pl.BlockSpec(memory_space=pltpu.VMEM)
    dma = lambda *shape: pltpu.SemaphoreType.DMA(shape)
    V = pltpu.VMEM
    return pl.pallas_call(
        layer_kernel,
        name="layer",
        out_shape=(
            jax.ShapeDtypeStruct((T, D), BF),
            jax.ShapeDtypeStruct((T, D), F32),
            jax.ShapeDtypeStruct((8, D), F32),
        )
        + tuple(jax.ShapeDtypeStruct((2, 2, ROWS[m], WIDE[m]), BF) for m in range(4)),
        in_specs=[anyspace] * 3 + [vmem, vmem, anyspace, anyspace, anyspace, vmem, anyspace, vmem],
        out_specs=(anyspace, anyspace, vmem) + (anyspace,) * 4,
        scratch_shapes=[
            pltpu.SMEM((1, T), jnp.int32), V((T, D), BF), V((2, T, D), BF), V((2, T, D), BF), V((T, D), F32),
            V((T, 128), F32), V((3, D, L), BF), V((L, D), BF), V((D, F), BF), V((F, D), BF), V((3, T, 128), F32),
            V((8, T, 256), BF), V((8, T, 256), BF), V((8, 128), jnp.int32), V((8, 8, 128), jnp.int32),
            pltpu.SMEM((8, 8, 128), jnp.int32), V((8 * T, 128), BF), V((8 * T, 128), BF), V((128, 8 * T), BF),
            V((2, 8 * T, T), F32), V((36 * T, T), BF), V((8, HD, T), F32), V((8, 2 * HD, T), BF),
            V((8, 2 * HD, T), BF), V((8, 2 * HD, T), BF), V((8, 2 * HD, T), BF), V((4, 2 * HD, T), BF),
            V((8, 2 * HD, T), BF), V((8, 2 * HD, T), BF), V((T, 1024), BF), V((2, T, 1024), BF), V((T, 1024), BF),
            V((2, T, 1024), BF), V((T, L), BF), V((2, T, L), BF), V((2, D, T), BF), V((2, 4, T, T), BF),
            V((2, 4, T, T), BF), V((2, 1024, 512), BF), V((2, 1024, 512), BF), V((2, 1024, 256), BF),
            V((2, 1024, 256), BF), V((3, 2, 256, 512), BF), V((3, 2, 256, 512), BF), V((3, 2, 256, 256), BF),
            V((3, 2, 256, 256), BF), V((3, 2, 256, 512), BF), V((3, 2, 256, 512), BF), V((3, 2, 256, 256), BF),
            V((3, 2, 256, 256), BF), V((4, 2, 32, 512), BF), V((4, 2, 32, 512), BF), V((8, 2, 32, 256), BF),
            V((8, 2, 32, 256), BF), V((2, 128, 512), BF), V((2, 128, 512), BF), V((2, 16, 256), BF),
            V((2, 16, 256), BF), V((2, 256, 512), BF), V((2, 256, 512), BF), V((2, 256, 256), BF),
            V((2, 256, 256), BF), V((7, 8, D), F32), V((7, 8, D), F32), V((T, D), BF), V((T, D), F32), dma(7),
            dma(6), dma(6), dma(4), dma(4), dma(2), dma(2), dma(4, 6), dma(4, 8), dma(4), dma(4), dma(4), dma(1),
            dma(7), dma(3),
        ],
        compiler_params=pltpu.CompilerParams(
            collective_id=0, has_side_effects=True, vmem_limit_bytes=63 * 2**20
        ),
    )(*args)


def widen_kernel(
    a, b, c, d, block, grads, small,
    fc_out, fc_in, qkv, out, block_out, tokens_grad, gain, bias, fc_in_bias, fc_out_bias,
    va, vb, vc, vd, wa, wb, wc, wd, vblk, vtgr, read, write,
):
    def reads(i):
        core, part = i // 4, i % 4
        rows = lambda n, k: pl.ds(pl.multiple_of(k * n, n), n)
        return (
            pltpu.make_async_copy(a.at[core, :, rows(256, part)], va.at[core, :, rows(256, part)], read.at[0, i]),
            pltpu.make_async_copy(b.at[:, :, rows(128, i)], vb.at[:, :, rows(128, i)], read.at[1, i]),
            pltpu.make_async_copy(c.at[:, :, rows(128, i)], vc.at[:, :, rows(128, i)], read.at[2, i]),
            pltpu.make_async_copy(d.at[:, 0, i // 2, rows(128, i % 2)], vd.at[:, 0, i // 2, rows(128, i % 2)], read.at[3, i]),
            pltpu.make_async_copy(d.at[core, 1, :, rows(64, part)], vd.at[core, 1, :, rows(64, part)], read.at[4, i]),
        )

    def issue(i, _):
        for copy in reads(i):
            copy.start()
        return 0

    lax.fori_loop(0, 8, issue, 0)
    two = [pltpu.make_async_copy(block, vblk, write.at[6]), pltpu.make_async_copy(grads, vtgr, write.at[7])]
    for copy in two:
        copy.start()
    gain[...] = small[0:1, :]
    bias[...] = small[1:2, :]
    fc_in_bias[:, 0:1024] = small[2:3, :]
    fc_in_bias[:, 1024:2048] = small[3:4, :]
    fc_out_bias[...] = small[4:5, :]

    def step(i, _):
        core, part = i // 4, i % 4
        copies = reads(i)
        copies[0].wait()
        here, there = pl.ds(pl.multiple_of(i * 256, 256), 256), pl.ds(pl.multiple_of(part * 256, 256), 256)
        for half in range(2):
            wa[here, 512 * half : 512 * half + 512] = va[core, half, there, :].astype(F32)
        pltpu.make_async_copy(wa.at[here], fc_out.at[here], write.at[0]).start()
        copies[1].wait()
        here = pl.ds(pl.multiple_of(i * 128, 128), 128)
        for k in range(2):
            for half in range(2):
                start = 1024 * k + 512 * half
                wb[here, start : start + 512] = vb[k, half, here, :].astype(F32)
        pltpu.make_async_copy(wb.at[here], fc_in.at[here], write.at[1]).start()
        copies[2].wait()
        copies[3].wait()
        there = pl.ds(pl.multiple_of(i % 2 * 128, 128), 128)
        for k in range(2):
            at = slice(256 * k, 256 * k + 256)
            wc[0, here, at] = vc[k, 0, here, :].astype(F32)
            wc[1, here, at] = vc[k, 1, here, :].astype(F32)
            wc[2, here, at] = vd[k, 0, i // 2, there, :].astype(F32)
        pltpu.make_async_copy(wc.at[:, here], qkv.at[:, here], write.at[2]).start()
        copies[4].wait()
        here, there = pl.ds(pl.multiple_of(i * 64, 64), 64), pl.ds(pl.multiple_of(part * 64, 64), 64)
        for k in range(4):
            wd[here, 256 * k : 256 * k + 256] = vd[core, 1, k, there, :].astype(F32)
        pltpu.make_async_copy(wd.at[here], out.at[here], write.at[3]).start()
        return 0

    lax.fori_loop(0, 8, step, 0)
    whole = [
        pltpu.make_async_copy(src, dst, write.at[i])
        for i, (src, dst) in enumerate(
            ((wa, fc_out), (wb, fc_in), (wc, qkv), (wd, out), (vblk, block_out), (vtgr, tokens_grad))
        )
    ]
    for i in range(2):
        two[i].wait()
        whole[4 + i].start()
    for copy in whole:
        copy.wait()


def call_widen(block, grads, small, a, b, c, d):
    shape, V = jax.ShapeDtypeStruct, pltpu.VMEM
    anyspace, vmem = pl.BlockSpec(memory_space=pl.ANY), pl.BlockSpec(memory_space=pltpu.VMEM)
    return pl.pallas_call(
        widen_kernel,
        name="widen",
        in_specs=[anyspace] * 6 + [vmem],
        out_specs=(anyspace,) * 6 + (vmem,) * 4,
        out_shape=(
            shape((F, D), F32), shape((D, F), F32), shape((3, D, L), F32), shape((L, D), F32),
            shape((T, D), BF), shape((T, D), F32),
            shape((1, D), F32), shape((1, D), F32), shape((1, F), F32), shape((1, D), F32),
        ),
        scratch_shapes=[
            V((2, 2, 1024, 512), BF), V((2, 2, 1024, 512), BF), V((2, 2, 1024, 256), BF), V((2, 2, 4, 256, 256), BF),
            V((F, D), F32), V((D, F), F32), V((3, D, L), F32), V((L, D), F32),
            V((T, D), BF), V((T, D), F32),
            pltpu.SemaphoreType.DMA((5, 8)), pltpu.SemaphoreType.DMA((8,)),
        ],
        compiler_params=pltpu.CompilerParams(vmem_limit_bytes=60 * 2**20),
    )(a, b, c, d.reshape(2, 2, 4, 256, 256), block, grads, small)


def local(
    tokens, positions, cotangent, ln_gain, ln_bias, qkv_weight, out_weight,
    fc_in_weight, fc_in_bias, fc_out_weight, fc_out_bias,
):
    parts = call_layer(
        positions,
        tokens[0],
        cotangent[0],
        ln_gain[None],
        ln_bias[None],
        qkv_weight.transpose(1, 0, 2),
        out_weight,
        fc_in_weight,
        fc_in_bias[None],
        fc_out_weight,
        fc_out_bias[None],
    )
    (
        fc_out_grad, fc_in_grad, qkv_grad, out_grad, block_out, tokens_grad,
        gain_grad, bias_grad, fc_in_bias_grad, fc_out_bias_grad,
    ) = call_widen(*parts)
    return (
        block_out[None],
        tokens_grad[None],
        gain_grad[0],
        bias_grad[0],
        qkv_grad.transpose(1, 0, 2),
        out_grad,
        fc_in_grad,
        fc_in_bias_grad[0],
        fc_out_grad,
        fc_out_bias_grad[0],
    )


def solution(mesh):
    placed = (
        P("seq", "ctx", None), P("seq", "ctx"), P("seq", "ctx", None), P(), P(),
        P(None, None, "tp"), P("tp", None), P(None, "tp"), P("tp"), P("tp", None), P(),
    )
    return jax.shard_map(
        local,
        mesh=mesh,
        in_specs=placed,
        out_specs=(
            P("seq", "ctx", None), P("seq", "ctx", None), P(), P(), P(None, None, "tp"),
            P("tp", None), P(None, "tp"), P("tp"), P("tp", None), P(),
        ),
        check_vma=False,
    )
```

```python
import math
from types import SimpleNamespace

import jax
import jax.numpy as jnp
from jax import lax
from jax.experimental import pallas as pl
from jax.experimental.pallas import tpu as pltpu
from jax.sharding import PartitionSpec as P

HD = 64
ROT = 32
T = 256
D = 1024
L = 512
F = 2048
MESH = pl.DeviceIdType.MESH
BF = jnp.bfloat16
F32 = jnp.float32
EPS = 1e-05
ROWS = (1024, 1024, 1024, 1024)
WIDE = (512, 512, 256, 256)
ORDER = ("xz", "xz", "xz", "xz")
Y_FIRST = (1, 1, 8, 8)


def dot(a, b):
    return lax.dot_general(a, b, (((1,), (0,)), ((), ())), preferred_element_type=F32)


def dot_nt(a, b):
    return lax.dot_general(a, b, (((1,), (1,)), ((), ())), preferred_element_type=F32)


def xor(a, b):
    return a + b - 2 * a * b


class Place:
    def __init__(self):
        seq, ctx, tp = lax.axis_index("seq"), lax.axis_index("ctx"), lax.axis_index("tp")
        self.seq, self.ctx, self.tp = seq, ctx, tp
        self.z, self.core, self.x, self.yh = seq // 2, seq % 2, ctx // 2, ctx % 2
        c, x, z = self.core, self.x, self.z
        flip = lambda i: i + 1 - 2 * (i % 2)
        self.sib = (z * 2 + 1 - c, ctx, tp)
        self.other_tp = (seq, ctx, 1 - tp)
        self.y = (seq, x * 2 + 1 - self.yh, tp)
        self.x_one = (seq, flip(x) * 2 + self.yh, tp)
        self.x_three = (seq, (3 - x) * 2 + self.yh, tp)
        self.z_one = (flip(z) * 2 + c, ctx, tp)
        self.z_three = ((3 - z) * 2 + c, ctx, tp)
        c = {"xz": c, "z": 1, "x": 0}
        self.order = [Order(self, c[kind]) for kind in ORDER]


class Order:
    def __init__(self, me, c):
        x, z = me.x, me.z
        pick = lambda a, b: tuple((1 - c) * p + c * q for p, q in zip(a, b))
        u, v = (1 - c) * x + c * z, (1 - c) * z + c * x
        one, three = pick(me.x_one, me.z_one), pick(me.x_three, me.z_three)
        self.before, self.after = (one, three), (three, one)
        flip = u + 1 - 2 * (u % 2)
        self.keep, self.give = (u, u), (3 - u, flip)
        self.their_give, self.their_keep = (lax.rem(u + 2, 4),) * 2, (flip, 3 - u)
        self.v = v
        self.others, self.seven = [], []
        for k in range(1, 4):
            to = lax.rem(v + k, 4)
            zz, xx = (1 - c) * to + c * z, (1 - c) * x + c * to
            self.others.append((to, (zz * 2 + me.core, xx * 2 + me.yh, me.tp)))
        self.place = v * 2 + me.yh
        for k in range(1, 8):
            to = lax.rem(self.place + k, 8)
            there = to // 2
            zz, xx = (1 - c) * there + c * z, (1 - c) * x + c * there
            self.seven.append((to, (zz * 2 + me.core, xx * 2 + to % 2, me.tp)))


def remote(src, dst, send, recv, device):
    return pltpu.make_async_remote_copy(
        src_ref=src, dst_ref=dst, send_sem=send, recv_sem=recv, device_id=device, device_id_type=MESH
    )


def rotate(u, cosine, even, odd):
    return u * cosine + pltpu.roll(u, 127, 1) * even + pltpu.roll(u, 1, 1) * odd


def keys(j):
    return slice(j * T, j * T + T)


def tri(r):
    return r * (r + 1) // 2 * T


def layer_kernel(
    pos_h, tok_h, cot_h, gain, lnb, wqkv_h, wout_h, fin_h, finb, fout_h, foutb,
    out_b, out_t, out_s, out_0, out_1, out_2, out_3,
    pos, tok, cot, nrm, xhat, inv, wqkv, wout, fin, fout, tabs, send1, land1, ptile, pland, psm, qg, kv,
    kvt, sbuf, pbuf, dvt, atts, aq, send2, land2, sib_att, send3, land3, act_o, act_b, gh_o, gh_b, lf_o,
    lf_b, nrm_t, tps, tpl, g0, g1, g2, g3, l0, l1, l2, l3, r0, r1, r2, r3, t0, t1, t2, t3, y0, y1, y2, y3,
    w0, w1, w2, w3, vs, vw, blk, tgr, in_sem, sib_s, sib_r, all_s, all_r, tp_s, tp_r, rs_s, rs_r, fw_s,
    fw_r, st_s, v_s, v_r, o_s,
):
    me = Place()
    core, ctx = me.core, me.ctx
    g, lands, res, outs = (g0, g1, g2, g3), (l0, l1, l2, l3), (r0, r1, r2, r3), (out_0, out_1, out_2, out_3)
    slots, ybuf, whole_q = (t0, t1, t2, t3), (y0, y1, y2, y3), (w0, w1, w2, w3)

    loads = [
        pltpu.make_async_copy(a, b, in_sem.at[i])
        for i, (a, b) in enumerate(
            (
                (pos_h, pos), (tok_h, tok), (cot_h, cot.at[0]), (wqkv_h, wqkv), (wout_h, wout),
                (fin_h, fin), (fout_h, fout),
            )
        )
    ]
    for copy in loads:
        copy.start()

    barrier = pltpu.get_barrier_semaphore()
    peers = [(me.seq, lax.rem(ctx + k, 8), me.tp) for k in range(1, 8)]
    across = [(lax.rem(me.z + k, 4) * 2 + core, me.x * 2 + yh, me.tp) for k in range(1, 4) for yh in range(2)]
    for device in peers + across + [me.sib, me.other_tp]:
        pl.semaphore_signal(barrier, inc=1, device_id=device, device_id_type=MESH)

    loads[1].wait()

    def norm_rows(i, _):
        rows = pl.ds(pl.multiple_of(i * 64, 64), 64)
        x = tok[rows, :].astype(F32)
        x = x - jnp.mean(x, axis=-1, keepdims=True)
        inv_std = lax.rsqrt(jnp.mean(x * x, axis=-1, keepdims=True) + EPS)
        x = x * inv_std
        xhat[rows, :] = x
        inv[rows, :] = jnp.broadcast_to(inv_std, (64, 128))
        nrm[0, rows, :] = (x * gain[...] + lnb[...]).astype(BF)
        return 0

    lax.fori_loop(0, T // 64, norm_rows, 0)

    loads[0].wait()
    first = pos[0, 0]
    lane = lax.broadcasted_iota(jnp.int32, (T, 128), 1)
    row = lax.broadcasted_iota(jnp.int32, (T, 128), 0)
    in_head = lane % HD
    low_lane = lane < HD
    freq = jnp.exp((in_head // 2).astype(F32) * (-2.0 * math.log(10000.0) / ROT))
    theta = (row + first).astype(F32) * freq
    turning = in_head < ROT
    sine = jnp.where(turning, jnp.sin(theta), 0.0)
    tabs[0] = jnp.where(turning, jnp.cos(theta), 1.0)
    tabs[1] = jnp.where(lane % 2 == 0, -sine, 0.0)
    tabs[2] = jnp.where(lane % 2 == 0, 0.0, sine)
    ptile[...] = jnp.full((8, 128), first, jnp.int32)

    loads[2].wait()
    pl.semaphore_wait(barrier, 15)

    sib_pairs = (
        (cot.at[0], cot.at[1]),
        (nrm.at[0], nrm.at[1]),
        (act_o, act_b.at[1]),
        (gh_o, gh_b.at[1]),
        (land2.at[pl.ds(4 * (1 - core), 4)], sib_att),
        (lf_o, lf_b.at[1]),
    )

    def to_sib(i):
        return remote(*sib_pairs[i], sib_s.at[i], sib_r.at[i], me.sib)

    def to_all(src, dst, i):
        for k in range(1, 8):
            to = lax.rem(ctx + k, 8)
            here = src if i == 0 else src.at[to]
            remote(here, dst.at[ctx], all_s.at[i], all_r.at[i], peers[k - 1]).start()
        dst[ctx] = src[...] if i == 0 else src[ctx]

    def all_seven(dst, i):
        return remote(dst.at[pl.ds(0, 7)], dst.at[pl.ds(0, 7)], all_s.at[i], all_r.at[i], me.sib)

    to_sib(0).start()
    to_sib(1).start()

    loads[3].wait()
    loads[4].wait()
    to_all(ptile, pland, 0)
    normed = nrm[0]
    swap = lambda a: pltpu.roll(a, HD, 1)
    for e in range(4):
        cols = slice(128 * e, 128 * e + 128)
        turn = (tabs[0], tabs[1], tabs[2])
        q = rotate(dot(normed, wqkv[0, :, cols]), *turn) * HD ** (-0.5)
        k = rotate(dot(normed, wqkv[1, :, cols]), *turn)
        v = dot(normed, wqkv[2, :, cols])
        ga = dot_nt(cot[0], wout[cols, :])
        send1[2 * e, :, 0:128] = jnp.where(low_lane, q, swap(ga)).astype(BF)
        send1[2 * e, :, 128:256] = jnp.where(low_lane, k, swap(v)).astype(BF)
        send1[2 * e + 1, :, 0:128] = jnp.where(low_lane, swap(q), ga).astype(BF)
        send1[2 * e + 1, :, 128:256] = jnp.where(low_lane, swap(k), v).astype(BF)
        for d in (2 * e, 2 * e + 1):

            @pl.when(ctx != d)
            def _():
                remote(send1.at[d], land1.at[ctx], all_s.at[1], all_r.at[1], (me.seq, d, me.tp)).start()

    land1[ctx] = send1[ctx]

    loads[5].wait()
    loads[6].wait()
    vs[0] = jnp.zeros((8, D), F32)

    def hidden(half, act_ref, gh_ref, i):
        start = pl.multiple_of(half * 1024 + i * 256, 256)
        here = pl.ds(pl.multiple_of(i * 256, 256), 256)
        u = dot(nrm[0], fin[:, pl.ds(start, 256)]) + finb[:, pl.ds(start, 256)]
        z = math.sqrt(2.0 / math.pi) * (u + 0.044715 * u * u * u)
        t = jnp.tanh(z)
        act_ref[:, here] = (0.5 * u * (1.0 + t)).astype(BF)
        slope = 0.5 * (1.0 + t) + (0.5 * math.sqrt(2.0 / math.pi)) * u * (1.0 - t * t) * (
            1.0 + 3 * 0.044715 * u * u
        )
        grad = dot_nt(cot[0], fout[pl.ds(start, 256), :]) * slope
        low = grad.astype(BF)
        gh_ref[:, here] = low
        vs[0, pl.ds(2 + half, 1), here] = jnp.sum(low.astype(F32), axis=0, keepdims=True)

    def other_half(i, _):
        hidden(1 - core, act_o, gh_o, i)
        return 0

    def own_half(i, _):
        hidden(core, act_b.at[0], gh_b.at[0], i)
        return 0

    lax.fori_loop(0, 4, other_half, 0)
    to_sib(2).start()
    to_sib(3).start()
    lax.fori_loop(0, 4, own_half, 0)

    def turn_over(src, dst):
        def body(i, _):
            here = pl.ds(pl.multiple_of(i * 128, 128), 128)
            for token in range(2):
                dst[token, here, :] = src[token, :, here].T
            return 0

        lax.fori_loop(0, D // 128, body, 0)

    def quarter(m, q):
        return pl.ds(pl.multiple_of(q * (ROWS[m] // 4), ROWS[m] // 4), ROWS[m] // 4)

    def swap_copy(m, h, k):
        o = me.order[m]
        q = (o.their_give, o.their_keep, o.give)[k][h]
        device = o.after[h] if k == 2 else o.before[h]
        return remote(g[m].at[h, quarter(m, q)], lands[m].at[k, h], rs_s.at[m, 0], rs_r.at[m, min(k, 1)], device)

    def arrived(m, ref, i):
        remote(ref, ref, rs_s.at[m, 0], rs_r.at[m, i], me.sib).wait_recv()

    def add(m, h, into, rows, start, *terms):
        block = 64

        def body(i, _):
            here = pl.ds(pl.multiple_of(i * block, block), block)
            total = g[m][h, pl.ds(pl.multiple_of(start + i * block, block), block), :].astype(F32)
            for k in terms:
                total = total + lands[m][k, h, here, :].astype(F32)
            if into is None:
                g[m][h, pl.ds(pl.multiple_of(start + i * block, block), block), :] = total.astype(BF)
            else:
                lands[m][into, h, here, :] = total.astype(BF)
            return 0

        lax.fori_loop(0, rows // block, body, 0)

    def first_sum(m):
        arrived(m, lands[m].at[0], 0)
        for h in range(2):
            add(m, h, None, ROWS[m] // 4, me.order[m].give[h] * (ROWS[m] // 4), 0)
            swap_copy(m, h, 2).start()

    def rows_of(m, v, y, wide):
        n = ROWS[m] // 32
        start = (y * 4 + v) * n if Y_FIRST[m] == 1 else (v * 2 + y) * n
        return pl.ds(pl.multiple_of(start, 16), n * wide)

    def along_v(m, ref, i, slot):
        o = me.order[m]
        for to, device in o.others:
            if slot:
                src = ref.at[:, rows_of(m, to, me.yh, 1) if Y_FIRST[m] == 1 else rows_of(m, to, 0, 2)]
                dst = slots[m].at[o.v]
            else:
                src = ref.at[:, rows_of(m, o.v, me.yh, 1) if Y_FIRST[m] == 1 else rows_of(m, o.v, 0, 2)]
                dst = src
            remote(src, dst, rs_s.at[m, i - 1], rs_r.at[m, i], device).start()

    def along_y(m, ref, i, slot):
        o = me.order[m]
        y = 1 - me.yh if slot else me.yh
        src = ref.at[:, rows_of(m, 0, y, 4) if Y_FIRST[m] == 1 else rows_of(m, o.v, y, 1)]
        remote(src, ybuf[m] if slot else src, rs_s.at[m, i - 1], rs_r.at[m, i], me.y).start()

    def sum_v(m, into):
        o = me.order[m]
        here = rows_of(m, o.v, me.yh, 1) if Y_FIRST[m] == 1 else rows_of(m, o.v, 0, 2)
        slots[m][o.v] = lands[m][2, :, here, :]
        for h in range(2):
            total = slots[m][0, h].astype(F32)
            for k in range(1, 4):
                total = total + slots[m][k, h].astype(F32)
            into[h, here, :] = total.astype(BF)

    def sum_y(m, into):
        here = rows_of(m, 0, me.yh, 4) if Y_FIRST[m] == 1 else rows_of(m, me.order[m].v, me.yh, 1)
        for h in range(2):
            total = lands[m][2, h, here, :].astype(F32) + ybuf[m][h].astype(F32)
            into[h, here, :] = total.astype(BF)

    def eighth(m, place):
        n = ROWS[m] // 32
        return pl.ds(pl.multiple_of(place * n, n), n)

    def sum_seven(m):
        arrived(m, slots[m].at[pl.ds(0, 7)], 2)
        o = me.order[m]
        here = eighth(m, o.place)
        slots[m][o.place] = lands[m][2, :, here, :]
        for h in range(2):
            total = slots[m][0, h].astype(F32)
            for k in range(1, 8):
                total = total + slots[m][k, h].astype(F32)
            whole_q[m][h, here, :] = total.astype(BF)
        piece = whole_q[m].at[:, here]
        for to, device in o.seven:
            remote(piece, piece, rs_s.at[m, 2], rs_r.at[m, 5], device).start()

    def three(m):
        return slots[m].at[pl.ds(0, 3)]

    def second_sum(m):
        arrived(m, lands[m].at[pl.ds(1, 2)], 1)
        for h in range(2):
            add(m, h, 2, ROWS[m] // 4, me.order[m].keep[h] * (ROWS[m] // 4), 1, 2)
        if Y_FIRST[m] == 8:
            o = me.order[m]
            for to, device in o.seven:
                piece = lands[m].at[2, :, eighth(m, to)]
                remote(piece, slots[m].at[o.place], rs_s.at[m, 1], rs_r.at[m, 2], device).start()
            return
        (along_y if Y_FIRST[m] == 1 else along_v)(m, lands[m].at[2], 2, True)

    def third_sum(m):
        if Y_FIRST[m] == 8:
            return sum_seven(m)
        arrived(m, ybuf[m] if Y_FIRST[m] == 1 else three(m), 2)
        (sum_y if Y_FIRST[m] == 1 else sum_v)(m, lands[m].at[2])
        (along_v if Y_FIRST[m] == 1 else along_y)(m, lands[m].at[2], 3, True)

    def fourth_sum(m):
        arrived(m, three(m) if Y_FIRST[m] == 1 else ybuf[m], 3)
        (sum_v if Y_FIRST[m] == 1 else sum_y)(m, whole_q[m])
        (along_v if Y_FIRST[m] == 1 else along_y)(m, whole_q[m], 4, False)

    def zeroth_gather(m):
        arrived(m, three(m) if Y_FIRST[m] == 1 else ybuf[m], 4)
        (along_y if Y_FIRST[m] == 1 else along_v)(m, whole_q[m], 5, False)

    def hand_over(m, h, src, q):
        there = outs[m].at[core, h, quarter(m, q)]
        remote(src, there, fw_s.at[m], fw_r.at[m], me.sib).start()
        pltpu.make_async_copy(src, there, st_s.at[m]).start()

    def spread(m, h, src, k):
        o = me.order[m]
        device = (o.before if k else o.after)[h]
        remote(src, res[m].at[k, h], rs_s.at[m, 5], rs_r.at[m, 6 + min(k, 1)], device).start()

    def first_gather(m):
        last = slots[m].at[pl.ds(0, 7)] if Y_FIRST[m] == 8 else ybuf[m] if Y_FIRST[m] == 1 else three(m)
        arrived(m, last, 5)
        o = me.order[m]
        for k in range(2):
            for h in range(2):
                spread(m, h, whole_q[m].at[h], k)
        for h in range(2):
            hand_over(m, h, whole_q[m].at[h], o.keep[h])

    def second_gather(m):
        arrived(m, lands[m].at[0], 6)
        o = me.order[m]
        for h in range(2):
            spread(m, h, res[m].at[0, h], 2)
            hand_over(m, h, res[m].at[0, h], o.give[h])

    def third_gather(m):
        arrived(m, lands[m].at[pl.ds(0, 2)], 7)
        o = me.order[m]
        for h in range(2):
            hand_over(m, h, res[m].at[1, h], o.their_keep[h])
            hand_over(m, h, res[m].at[2, h], o.their_give[h])

    def outer(m, left_t, right):
        o = me.order[m]
        for k, qs in enumerate((o.their_give, o.their_keep, o.give, o.keep)):
            for h in range(2):
                rows = quarter(m, qs[h])
                cols = slice(WIDE[m] * h, WIDE[m] * h + WIDE[m])
                total = dot(left_t[0, rows, :], right[0, :, cols]) + dot(left_t[1, rows, :], right[1, :, cols])
                g[m][h, rows, :] = total.astype(BF)
                if k < 2:
                    swap_copy(m, h, k).start()

    act_t = pbuf.at[pl.ds(0, 2 * D)].reshape(2, D, T)
    to_sib(2).wait_recv()
    turn_over(act_b, act_t)
    to_sib(0).wait_recv()
    outer(0, act_t, cot)
    to_sib(1).wait_recv()
    turn_over(nrm, nrm_t)
    to_sib(3).wait_recv()
    outer(1, nrm_t, gh_b)
    vs[0, 4:5, :] = jnp.sum(cot[0].astype(F32), axis=0, keepdims=True)

    all_seven(pland, 0).wait_recv()
    to_scalar = pltpu.make_async_copy(pland, psm, o_s.at[2])
    to_scalar.start()
    all_seven(land1, 1).wait_recv()
    to_scalar.wait()
    rank = [psm[c, 0, 0] // T for c in range(8)]
    for r in range(8):
        at = 0
        for c in range(8):
            at = jnp.where(rank[c] == r, c, at)
        block = land1[at]
        qg[keys(r), :] = block[:, 0:128]
        kv[keys(r), :] = block[:, 128:256]
        kvt[:, keys(r)] = block[:, 128:256].T

    causal = lax.broadcasted_iota(jnp.int32, (T, T), 0) <= lax.broadcasted_iota(jnp.int32, (T, T), 1)
    deltas = [None] * 8

    def split(r):
        both_lanes = qg[keys(r), :]
        zero = jnp.zeros_like(both_lanes)
        return jnp.where(low_lane, both_lanes, zero), jnp.where(low_lane, zero, both_lanes)

    def scores(r):
        q, _ = split(r)
        top = jnp.full((8, T), -1e30, F32)
        for j in range(r + 1):
            s = dot_nt(kv[keys(j), :], q)
            if j == r:
                s = jnp.where(causal, s, -1e30)
            sbuf[r % 2, keys(j), :] = s
            top = jnp.maximum(top, jnp.max(s.reshape(T // 8, 8, T), axis=0))
        return top

    def weigh(r, top):
        top = jnp.max(top, axis=0, keepdims=True)
        total, att = jnp.zeros((8, T), F32), jnp.zeros((HD, T), F32)
        for j in range(r + 1):
            e = jnp.exp(sbuf[r % 2, keys(j), :] - top)
            total = total + jnp.sum(e.reshape(T // 8, 8, T), axis=0)
            low = e.astype(BF)
            pbuf[tri(r) + j * T : tri(r) + j * T + T, :] = low
            att = att + dot(kvt[HD:, keys(j)], low)
        scale = 1.0 / jnp.sum(total, axis=0, keepdims=True)
        att = att * scale
        atts[r, 0:HD, :] = att.astype(BF)
        both_lanes = qg[keys(r), :]
        ga_t = (both_lanes.T.astype(F32)[HD:, :] * scale).astype(BF)
        deltas[r] = jnp.sum(ga_t.astype(F32) * att, axis=0, keepdims=True)
        ga = jnp.concatenate([jnp.zeros((HD, T), BF), ga_t], axis=0).T
        qg[keys(r), :] = jnp.where(low_lane, both_lanes, ga)
        for j in range(r + 1):
            update = dot_nt(ga_t, pbuf[tri(r) + j * T : tri(r) + j * T + T, :])
            if r == 7:
                dvt[j] = update
            else:
                dvt[j] += update
        atts[r, HD:, :] = dvt[r].astype(BF)

    def back(r):
        _, ga = split(r)
        q_t = qg[keys(r), :].T[0:HD, :]
        dq = jnp.zeros((HD, T), F32)
        for j in range(r + 1):
            prob = pbuf[tri(r) + j * T : tri(r) + j * T + T, :]
            dp = dot_nt(kv[keys(j), :], ga)
            ds = (prob.astype(F32) * (dp - deltas[r])).astype(BF)
            update = dot_nt(q_t, ds)
            if r == 7:
                sbuf[0, j * HD : j * HD + HD, :] = update
            else:
                sbuf[0, j * HD : j * HD + HD, :] += update
            dq = dq + dot(kvt[:HD, keys(j)], ds)
        aq[r, 0:HD, :] = (dq * HD ** (-0.5)).astype(BF)
        aq[r, HD:, :] = sbuf[0, r * HD : r * HD + HD, :].astype(BF)

    own, oth = pl.multiple_of(core * 1024, 1024), pl.multiple_of((1 - core) * 1024, 1024)

    def tp_copy(i, j):
        return remote(tps.at[i, j], tpl.at[i, j], tp_s.at[i], tp_r.at[i], me.other_tp)

    def tp_all(i):
        return remote(tps.at[i], tpl.at[i], tp_s.at[i], tp_r.at[i], me.other_tp)

    def mixed(i, _):
        cols = pl.ds(pl.multiple_of(i * 256, 256), 256)
        grad = dot_nt(gh_b[0], fin[cols, pl.ds(own, 1024)]) + dot_nt(gh_o[...], fin[cols, pl.ds(oth, 1024)])
        sbuf[1, cols, :] = grad + dot_nt(lf_b[0], wqkv[2, cols, :])
        return 0

    def gather_heads(half, ref):
        turn = (tabs[0], -tabs[1], -tabs[2])
        for e in range(2):
            low, high = 4 * half + 2 * e, 4 * half + 2 * e + 1
            for j in range(2):
                rows = slice(HD * j, HD * j + HD)
                pair = jnp.concatenate([land3[low, rows, :], land3[high, rows, :]], axis=0)
                part = rotate(pair.T.astype(F32), *turn)
                ref[:, 256 * j + 128 * e : 256 * j + 128 * e + 128] = part.astype(BF)

    def late(i, _):
        cols = pl.ds(pl.multiple_of(i * 256, 256), 256)
        grad = sbuf[1, cols, :]
        for ref, half in ((lf_b.at[0], core), (lf_o, 1 - core)):
            at = pl.multiple_of(half * 256, 256)
            for j in range(2):
                grad = grad + dot_nt(ref[:, 256 * j : 256 * j + 256], wqkv[j, cols, pl.ds(at, 256)])
        tps[1, i] = grad.astype(BF)
        vs[0, 0:1, cols] = jnp.sum(grad * xhat[:, cols], axis=0, keepdims=True)
        vs[0, 1:2, cols] = jnp.sum(grad, axis=0, keepdims=True)
        return 0

    v_to = (me.sib, me.y, me.x_one, me.x_three, me.z_one, me.z_three, me.other_tp)

    def v_copy(i):
        return remote(vs.at[i], vw.at[i], v_s.at[0], v_r.at[i], v_to[i])

    def v_step(i):
        v_copy(i).wait_recv()
        total = vs[i] + vw[i]
        if i == 6:
            here = lax.broadcasted_iota(jnp.int32, (8, D), 0) < 2
            out_s[...] = jnp.where(here, total, vs[i])
        else:
            vs[i + 1] = total
            v_copy(i + 1).start()

    def finish(i, _):
        rows = pl.ds(pl.multiple_of(i * 32, 32), 32)

        def whole(k):
            parts = [tps[k, j, rows, :].astype(F32) + tpl[k, j, rows, :].astype(F32) for j in range(4)]
            return jnp.concatenate(parts, axis=1).astype(BF).astype(F32)

        blk[rows, :] = (tok[rows, :].astype(F32) + whole(0) + foutb[...]).astype(BF)
        grad = whole(1)
        scaled = grad * gain[...]
        x = xhat[rows, :]
        mean_one = jnp.mean(scaled, axis=-1, keepdims=True)
        mean_two = jnp.mean(scaled * x, axis=-1, keepdims=True)
        inv_std = inv[rows, 0:1]
        tgr[rows, :] = cot[0, rows, :].astype(F32) + inv_std * (scaled - mean_one - x * mean_two)
        return 0

    to_out = [pltpu.make_async_copy(blk, out_b, o_s.at[0]), pltpu.make_async_copy(tgr, out_t, o_s.at[1])]

    def branch(i, _):
        cols = pl.ds(pl.multiple_of(i * 256, 256), 256)
        part = dot(act_b[0], fout[pl.ds(own, 1024), cols]) + dot(act_o[...], fout[pl.ds(oth, 1024), cols])
        tps[0, i] = (part + dot(lf_o[...], wout[:, cols])).astype(BF)
        return 0

    first_sum(0)
    ahead = scores(7)
    for r in range(7, -1, -1):
        now = ahead
        if r:
            ahead = scores(r - 1)
        weigh(r, now)
    for c in range(8):
        send2[c] = atts[rank[c]]
    to_all(send2, land2, 2)
    back(7)
    back(6)
    back(5)
    back(4)
    first_sum(1)
    back(3)
    back(2)
    second_sum(0)
    back(1)
    back(0)
    for c in range(8):
        send3[c] = aq[rank[c]]
    to_all(send3, land3, 3)
    all_seven(land2, 2).wait_recv()
    to_sib(4).start()
    lf_o[...] = land2[:, 0:HD, :].reshape(L, T).T
    lf_b[0] = land2[:, HD:, :].reshape(L, T).T
    lax.fori_loop(0, 4, branch, 0)
    second_sum(1)
    to_sib(4).wait_recv()
    four = pl.ds(4 * core, 4)
    o3 = me.order[3]
    for k in range(4):
        for h in range(2):
            q = (o3.their_give, o3.their_keep, o3.give, o3.keep)[k][h]
            rows = quarter(3, q)
            if h == 0:
                total = dot_nt(nrm_t[0, rows, :], land2[four, HD:, :].reshape(T, T))
                total = total + dot_nt(nrm_t[1, rows, :], sib_att[:, HD:, :].reshape(T, T))
            else:
                total = dot(land2[four, 0:HD, :].reshape(T, T), cot[0, :, rows])
                total = total + dot(sib_att[:, 0:HD, :].reshape(T, T), cot[1, :, rows])
            g3[h, rows, :] = total.astype(BF)
            if k < 2:
                swap_copy(3, h, k).start()
    tp_copy(0, 0).start()
    third_sum(0)
    lax.fori_loop(0, 4, mixed, 0)
    all_seven(land3, 3).wait_recv()
    gather_heads(1 - core, lf_o)
    to_sib(5).start()
    gather_heads(core, lf_b.at[0])
    lax.fori_loop(0, 4, late, 0)
    v_copy(0).start()
    first_sum(3)
    fourth_sum(0)
    tp_copy(1, 3).start()
    third_sum(1)
    to_sib(5).wait_recv()
    outer(2, nrm_t, lf_b)
    v_step(0)
    second_sum(3)
    zeroth_gather(0)
    v_step(1)
    first_sum(2)
    fourth_sum(1)
    third_sum(3)
    v_step(2)
    first_gather(0)
    second_sum(2)
    zeroth_gather(1)
    first_gather(3)
    v_step(3)
    second_gather(0)
    third_sum(2)
    tp_copy(1, 2).start()
    tp_copy(0, 2).start()
    tp_copy(0, 1).start()
    tp_copy(1, 0).start()
    second_gather(3)
    tp_copy(1, 1).start()
    tp_copy(0, 3).start()
    v_step(4)
    first_gather(1)
    first_gather(2)
    v_step(5)
    third_gather(3)
    second_gather(1)
    third_gather(0)
    second_gather(2)
    v_step(6)
    third_gather(1)
    tp_all(0).wait_recv()
    tp_all(1).wait_recv()
    lax.fori_loop(0, T // 32, finish, 0)
    to_out[0].start()
    to_out[1].start()
    third_gather(2)
    for m in range(4):
        one, other = (ybuf[m], three(m)) if Y_FIRST[m] == 1 else (three(m), ybuf[m])
        every = (lands[m], one, other, other, one, lands[m])
        if Y_FIRST[m] == 8:
            seven = slots[m].at[pl.ds(0, 7)]
            every = (lands[m], seven, seven, None, None, lands[m])
        for i, ref in enumerate(every):
            if ref is None:
                continue
            remote(ref, ref, rs_s.at[m, i], rs_r.at[m, 0], me.sib).wait_send()
        half_out = outs[m].at[1 - core]
        remote(g[m], half_out, fw_s.at[m], fw_r.at[m], me.sib).wait()
        pltpu.make_async_copy(g[m], outs[m].at[core], st_s.at[m]).wait()
    for i in range(6):
        to_sib(i).wait_send()
    all_seven(pland, 0).wait_send()
    all_seven(land1, 1).wait_send()
    all_seven(land2, 2).wait_send()
    all_seven(land3, 3).wait_send()
    for i in range(2):
        tp_all(i).wait_send()
        to_out[i].wait()
    remote(vs, vw, v_s.at[0], v_r.at[0], me.sib).wait_send()


def call_layer(*args):
    anyspace = pl.BlockSpec(memory_space=pl.ANY)
    vmem = pl.BlockSpec(memory_space=pltpu.VMEM)
    dma = lambda *shape: pltpu.SemaphoreType.DMA(shape)
    V = pltpu.VMEM
    return pl.pallas_call(
        layer_kernel,
        name="layer",
        out_shape=(
            jax.ShapeDtypeStruct((T, D), BF),
            jax.ShapeDtypeStruct((T, D), F32),
            jax.ShapeDtypeStruct((8, D), F32),
        )
        + tuple(jax.ShapeDtypeStruct((2, 2, ROWS[m], WIDE[m]), BF) for m in range(4)),
        in_specs=[anyspace] * 3 + [vmem, vmem, anyspace, anyspace, anyspace, vmem, anyspace, vmem],
        out_specs=(anyspace, anyspace, vmem) + (anyspace,) * 4,
        scratch_shapes=[
            pltpu.SMEM((1, T), jnp.int32), V((T, D), BF), V((2, T, D), BF), V((2, T, D), BF), V((T, D), F32),
            V((T, 128), F32), V((3, D, L), BF), V((L, D), BF), V((D, F), BF), V((F, D), BF), V((3, T, 128), F32),
            V((8, T, 256), BF), V((8, T, 256), BF), V((8, 128), jnp.int32), V((8, 8, 128), jnp.int32),
            pltpu.SMEM((8, 8, 128), jnp.int32), V((8 * T, 128), BF), V((8 * T, 128), BF), V((128, 8 * T), BF),
            V((2, 8 * T, T), F32), V((36 * T, T), BF), V((8, HD, T), F32), V((8, 2 * HD, T), BF),
            V((8, 2 * HD, T), BF), V((8, 2 * HD, T), BF), V((8, 2 * HD, T), BF), V((4, 2 * HD, T), BF),
            V((8, 2 * HD, T), BF), V((8, 2 * HD, T), BF), V((T, 1024), BF), V((2, T, 1024), BF), V((T, 1024), BF),
            V((2, T, 1024), BF), V((T, L), BF), V((2, T, L), BF), V((2, D, T), BF), V((2, 4, T, T), BF),
            V((2, 4, T, T), BF), V((2, 1024, 512), BF), V((2, 1024, 512), BF), V((2, 1024, 256), BF),
            V((2, 1024, 256), BF), V((3, 2, 256, 512), BF), V((3, 2, 256, 512), BF), V((3, 2, 256, 256), BF),
            V((3, 2, 256, 256), BF), V((3, 2, 256, 512), BF), V((3, 2, 256, 512), BF), V((3, 2, 256, 256), BF),
            V((3, 2, 256, 256), BF), V((4, 2, 32, 512), BF), V((4, 2, 32, 512), BF), V((8, 2, 32, 256), BF),
            V((8, 2, 32, 256), BF), V((2, 128, 512), BF), V((2, 128, 512), BF), V((2, 16, 256), BF),
            V((2, 16, 256), BF), V((2, 256, 512), BF), V((2, 256, 512), BF), V((2, 256, 256), BF),
            V((2, 256, 256), BF), V((7, 8, D), F32), V((7, 8, D), F32), V((T, D), BF), V((T, D), F32), dma(7),
            dma(6), dma(6), dma(4), dma(4), dma(2), dma(2), dma(4, 6), dma(4, 8), dma(4), dma(4), dma(4), dma(1),
            dma(7), dma(3),
        ],
        compiler_params=pltpu.CompilerParams(
            collective_id=0, has_side_effects=True, vmem_limit_bytes=63 * 2**20
        ),
    )(*args)


def widen_kernel(
    a, b, c, d, block, grads, small,
    fc_out, fc_in, qkv, out, block_out, tokens_grad, gain, bias, fc_in_bias, fc_out_bias,
    va, vb, vc, vd, wa, wb, wc, wd, vblk, vtgr, read, write,
):
    def reads(i):
        core, part = i // 4, i % 4
        rows = lambda n, k: pl.ds(pl.multiple_of(k * n, n), n)
        return (
            pltpu.make_async_copy(a.at[core, :, rows(256, part)], va.at[core, :, rows(256, part)], read.at[0, i]),
            pltpu.make_async_copy(b.at[:, :, rows(128, i)], vb.at[:, :, rows(128, i)], read.at[1, i]),
            pltpu.make_async_copy(c.at[:, :, rows(128, i)], vc.at[:, :, rows(128, i)], read.at[2, i]),
            pltpu.make_async_copy(d.at[:, 0, i // 2, rows(128, i % 2)], vd.at[:, 0, i // 2, rows(128, i % 2)], read.at[3, i]),
            pltpu.make_async_copy(d.at[core, 1, :, rows(64, part)], vd.at[core, 1, :, rows(64, part)], read.at[4, i]),
        )

    def issue(i, _):
        for copy in reads(i):
            copy.start()
        return 0

    lax.fori_loop(0, 8, issue, 0)
    two = [pltpu.make_async_copy(block, vblk, write.at[6]), pltpu.make_async_copy(grads, vtgr, write.at[7])]
    for copy in two:
        copy.start()
    gain[...] = small[0:1, :]
    bias[...] = small[1:2, :]
    fc_in_bias[:, 0:1024] = small[2:3, :]
    fc_in_bias[:, 1024:2048] = small[3:4, :]
    fc_out_bias[...] = small[4:5, :]

    def step(i, _):
        core, part = i // 4, i % 4
        copies = reads(i)
        copies[0].wait()
        here, there = pl.ds(pl.multiple_of(i * 256, 256), 256), pl.ds(pl.multiple_of(part * 256, 256), 256)
        for half in range(2):
            wa[here, 512 * half : 512 * half + 512] = va[core, half, there, :].astype(F32)
        pltpu.make_async_copy(wa.at[here], fc_out.at[here], write.at[0]).start()
        copies[1].wait()
        here = pl.ds(pl.multiple_of(i * 128, 128), 128)
        for k in range(2):
            for half in range(2):
                start = 1024 * k + 512 * half
                wb[here, start : start + 512] = vb[k, half, here, :].astype(F32)
        pltpu.make_async_copy(wb.at[here], fc_in.at[here], write.at[1]).start()
        copies[2].wait()
        copies[3].wait()
        there = pl.ds(pl.multiple_of(i % 2 * 128, 128), 128)
        for k in range(2):
            at = slice(256 * k, 256 * k + 256)
            wc[0, here, at] = vc[k, 0, here, :].astype(F32)
            wc[1, here, at] = vc[k, 1, here, :].astype(F32)
            wc[2, here, at] = vd[k, 0, i // 2, there, :].astype(F32)
        pltpu.make_async_copy(wc.at[:, here], qkv.at[:, here], write.at[2]).start()
        copies[4].wait()
        here, there = pl.ds(pl.multiple_of(i * 64, 64), 64), pl.ds(pl.multiple_of(part * 64, 64), 64)
        for k in range(4):
            wd[here, 256 * k : 256 * k + 256] = vd[core, 1, k, there, :].astype(F32)
        pltpu.make_async_copy(wd.at[here], out.at[here], write.at[3]).start()
        return 0

    lax.fori_loop(0, 8, step, 0)
    whole = [
        pltpu.make_async_copy(src, dst, write.at[i])
        for i, (src, dst) in enumerate(
            ((wa, fc_out), (wb, fc_in), (wc, qkv), (wd, out), (vblk, block_out), (vtgr, tokens_grad))
        )
    ]
    for i in range(2):
        two[i].wait()
        whole[4 + i].start()
    for copy in whole:
        copy.wait()


def call_widen(block, grads, small, a, b, c, d):
    shape, V = jax.ShapeDtypeStruct, pltpu.VMEM
    anyspace, vmem = pl.BlockSpec(memory_space=pl.ANY), pl.BlockSpec(memory_space=pltpu.VMEM)
    return pl.pallas_call(
        widen_kernel,
        name="widen",
        in_specs=[anyspace] * 6 + [vmem],
        out_specs=(anyspace,) * 6 + (vmem,) * 4,
        out_shape=(
            shape((F, D), F32), shape((D, F), F32), shape((3, D, L), F32), shape((L, D), F32),
            shape((T, D), BF), shape((T, D), F32),
            shape((1, D), F32), shape((1, D), F32), shape((1, F), F32), shape((1, D), F32),
        ),
        scratch_shapes=[
            V((2, 2, 1024, 512), BF), V((2, 2, 1024, 512), BF), V((2, 2, 1024, 256), BF), V((2, 2, 4, 256, 256), BF),
            V((F, D), F32), V((D, F), F32), V((3, D, L), F32), V((L, D), F32),
            V((T, D), BF), V((T, D), F32),
            pltpu.SemaphoreType.DMA((5, 8)), pltpu.SemaphoreType.DMA((8,)),
        ],
        compiler_params=pltpu.CompilerParams(vmem_limit_bytes=60 * 2**20),
    )(a, b, c, d.reshape(2, 2, 4, 256, 256), block, grads, small)


def local(
    tokens, positions, cotangent, ln_gain, ln_bias, qkv_weight, out_weight,
    fc_in_weight, fc_in_bias, fc_out_weight, fc_out_bias,
):
    parts = call_layer(
        positions,
        tokens[0],
        cotangent[0],
        ln_gain[None],
        ln_bias[None],
        qkv_weight.transpose(1, 0, 2),
        out_weight,
        fc_in_weight,
        fc_in_bias[None],
        fc_out_weight,
        fc_out_bias[None],
    )
    (
        fc_out_grad, fc_in_grad, qkv_grad, out_grad, block_out, tokens_grad,
        gain_grad, bias_grad, fc_in_bias_grad, fc_out_bias_grad,
    ) = call_widen(*parts)
    return (
        block_out[None],
        tokens_grad[None],
        gain_grad[0],
        bias_grad[0],
        qkv_grad.transpose(1, 0, 2),
        out_grad,
        fc_in_grad,
        fc_in_bias_grad[0],
        fc_out_grad,
        fc_out_bias_grad[0],
    )


def solution(mesh):
    placed = (
        P("seq", "ctx", None), P("seq", "ctx"), P("seq", "ctx", None), P(), P(),
        P(None, None, "tp"), P("tp", None), P(None, "tp"), P("tp"), P("tp", None), P(),
    )
    return jax.shard_map(
        local,
        mesh=mesh,
        in_specs=placed,
        out_specs=(
            P("seq", "ctx", None), P("seq", "ctx", None), P(), P(), P(None, None, "tp"),
            P("tp", None), P(None, "tp"), P("tp"), P("tp", None), P(),
        ),
        check_vma=False,
    )
```
